32 devices in a mesh: space: 8 (over z, y), chan: 4 (over x, core).
Axes of the slice: x: 2, y: 2, z: 4, core: 2. Of those that a mesh axis runs over, the one named last changes fastest.
Arguments:
- features: bfloat16 [16384, 256], P('space', 'chan'), may hold values from -6 to 6
- kernel_map: int32 [8, 27, 16, 3], P('space'), may hold values from 0 to 15, as said below
- block_count: int32 [8], replicated, may hold values from 3 to 16, as said below
- weight_one: bfloat16 [27, 256, 256], P(None, 'chan'), may hold values from -0.078125 to 0.078125
- weight_two: bfloat16 [27, 256, 256], P(None, 'chan'), may hold values from -0.078125 to 0.078125
- cotangent: bfloat16 [16384, 256], P('space', 'chan'), may hold values from -0.026977539 to 0.026977539
Outputs:
- output: bfloat16 [16384, 256], P('space', 'chan')
- grad_one: float32 [27, 256, 256], P(None, 'chan', 'space')
- grad_two: float32 [27, 256, 256], P(None, 'chan', 'space')
The draws below stay inside these ranges and needn't reach their ends.
Inputs may be any that keep to these rules, and one draw needn't show every extreme that they name: `kernel_map`: column 0 of slab s's entries is s - 1, s or s + 1. Column 1 is a block below block_count of that source slab; from slab s - 1 it is one of that slab's last 2 live blocks, from slab s + 1 one of its first 2. Column 2 lies below 16. Entries stand in offset order, 16 per offset and slab. `block_count`: at least one slab has all 16 blocks live.
All inputs are finite; a program needn't handle non-finite values.
Results may differ from the reference program's by a relative error of at most 0.015.
Values may be sent and summed in bfloat16 or wider, within the bound.
No kernel may reach another device: no remote copies, remote signals or barrier semaphores. Data moves between devices by JAX's collectives and lax.ppermute only.
A program may use at most 64 MiB of HBM per device.

```python
import jax
import jax.numpy as jnp
from jax import lax

C = 256
KVOL = 27
BLK = 128
HB = 2
BLK_DEV = 16
EPK = 16
ROWS = 16384
N_SPACE = 8


def shared_counts(key):
    inner = jax.random.fold_in(key, 7)
    key_a, key_b, key_c = jax.random.split(inner, 3)
    lowest = HB + 1
    spread = BLK_DEV - lowest
    first = jax.random.randint(key_a, (N_SPACE,), 0, spread + 1)
    second = jax.random.randint(key_b, (N_SPACE,), 0, spread + 1)
    counts = lowest + first * second // spread
    fullest = jax.random.randint(key_c, (), 0, N_SPACE)
    return jnp.where(jnp.arange(N_SPACE) == fullest, BLK_DEV, counts).astype(jnp.int32)


def draw_block_count(key, part):
    return shared_counts(key)


def draw_kernel_map(key, part):
    counts = shared_counts(key)
    inner = jax.random.fold_in(key, 11)
    key_a, key_b, key_c = jax.random.split(inner, 3)
    shape = (N_SPACE, KVOL, EPK)
    shard = jnp.broadcast_to(jnp.arange(N_SPACE, dtype=jnp.int32)[:, None, None], shape)
    pick = jax.random.randint(key_a, shape, 0, 8)
    offset = jnp.where(pick == 0, -1, jnp.where(pick == 1, 1, 0))
    source = jnp.clip(shard + offset, 0, N_SPACE - 1)
    source_count = counts[source]
    fraction = jax.random.randint(key_b, shape, 0, 1048576)
    same_block = fraction * source_count // 1048576
    rim_block = fraction * HB // 1048576
    block = jnp.where(source == shard, same_block, jnp.where(source < shard, source_count - HB + rim_block, rim_block))
    target = jax.random.randint(key_c, shape, 0, BLK_DEV)
    return jnp.stack([source, block, target], -1).astype(jnp.int32)


def level_of(key, shape, shards, least, top_value):
    loudness, own = 1.0, jax.random.fold_in(key, 6)
    for position, blocks in shards:
        heights = jnp.exp(jax.random.uniform(jax.random.fold_in(own, position), (blocks,), jnp.float32, least / len(shards), top_value / len(shards)))
        loudness = loudness * jnp.repeat(heights, shape[position] // blocks).reshape([-1 if axis == position else 1 for axis in range(len(shape))])
    return loudness


def scatter_about(stream_key, extent, scale, most, pieces=(), kind=jnp.bfloat16):
    array = scale * jax.random.normal(stream_key, extent, jnp.float32)
    if pieces:
        array = array * level_of(stream_key, extent, pieces, -0.22, 0.18)
    return jnp.clip(array, -most, most).astype(kind)


def setup_inputs(seed: int = 0) -> dict:
    splits = jax.random.split(jax.random.key(seed), 7)
    features = scatter_about(splits[0], (ROWS, C), 1.0, 6.0, ((0, 8), (1, 4)))
    kernel_map = draw_kernel_map(jax.random.fold_in(splits[6], 71), 0)
    block_count = draw_block_count(jax.random.fold_in(splits[6], 71), 0)
    weight_one = scatter_about(splits[3], (KVOL, C, C), (C * KVOL * EPK // BLK_DEV) ** -0.5, 0.078125, ((1, 4),))
    weight_two = scatter_about(splits[4], (KVOL, C, C), (C * KVOL * EPK // BLK_DEV) ** -0.5, 0.078125, ((1, 4),))
    cotangent = scatter_about(splits[5], (ROWS, C), 0.0045, 0.026977539, ((0, 8), (1, 4)))
    return {"features": features, "kernel_map": kernel_map, "block_count": block_count, "weight_one": weight_one, "weight_two": weight_two, "cotangent": cotangent}


def entry_tables(kernel_map, block_count, shard):
    entry = kernel_map[shard]
    source = (entry[..., 0] * BLK_DEV + entry[..., 1]).astype(jnp.int32)
    live = entry[..., 2] < block_count[shard]
    choose = ((entry[..., 2][..., None] == jnp.arange(BLK_DEV, dtype=jnp.int32)) & live[..., None]).astype(jnp.float32)
    return source, choose


def convolve(feat, weights, kernel_map, block_count):
    blocks = feat.reshape(N_SPACE * BLK_DEV, BLK, C)
    kernel = weights.astype(jnp.float32)

    def one(shard):
        source, choose = entry_tables(kernel_map, block_count, shard)
        picked = blocks[source].astype(jnp.float32)
        prod = jnp.einsum("kerc,kdc->kerd", picked, kernel)
        return jnp.einsum("keb,kerd->brd", choose, prod)

    out = lax.map(one, jnp.arange(N_SPACE, dtype=jnp.int32))
    return out.reshape(ROWS, C)


def backward_pass(feat, grads, weights, kernel_map, block_count, want_input):
    blocks = feat.reshape(N_SPACE * BLK_DEV, BLK, C)
    grad_blocks = grads.astype(jnp.float32).reshape(N_SPACE, BLK_DEV, BLK, C)
    kernel = weights.astype(jnp.float32)

    def step(carry, shard):
        wsum, isum = carry
        source, choose = entry_tables(kernel_map, block_count, shard)
        picked = blocks[source].astype(jnp.float32)
        chosen = jnp.einsum("keb,brd->kerd", choose, grad_blocks[shard])
        wsum = wsum + jnp.einsum("kerc,kerd->kdc", picked, chosen)
        if want_input:
            contrib = jnp.einsum("kerd,kdc->kerc", chosen, kernel)
            isum = isum.at[source.reshape(-1)].add(contrib.reshape(-1, BLK, C))
        return (wsum, isum), None

    init_w = jnp.zeros((KVOL, C, C), jnp.float32)
    if want_input:
        init_i = jnp.zeros((N_SPACE * BLK_DEV, BLK, C), jnp.float32)
    else:
        init_i = jnp.zeros((1,), jnp.float32)
    (wsum, isum), _ = lax.scan(step, (init_w, init_i), jnp.arange(N_SPACE, dtype=jnp.int32))
    return wsum, isum


def reference(features, kernel_map, block_count, weight_one, weight_two, cotangent):
    z_one = convolve(features, weight_one, kernel_map, block_count)
    hidden = jax.nn.silu(z_one).astype(jnp.bfloat16)
    output = convolve(hidden, weight_two, kernel_map, block_count).astype(jnp.bfloat16)
    grad_two, grad_hidden = backward_pass(hidden, cotangent, weight_two, kernel_map, block_count, True)
    grad_hidden = grad_hidden.reshape(ROWS, C)
    gate = jax.nn.sigmoid(z_one)
    grad_z = (grad_hidden * gate * (1.0 + z_one * (1.0 - gate))).astype(jnp.bfloat16)
    grad_one, _ = backward_pass(features, grad_z, weight_one, kernel_map, block_count, False)
    return output, grad_one, grad_two
```

```python
import functools

import jax
import jax.numpy as jnp
from jax import lax
from jax.experimental import pallas as pl
from jax.experimental.pallas import tpu as pltpu
from jax.sharding import PartitionSpec as P

BLK = 128
HB = 2
RIM = HB * BLK
STEP = 256
F32 = jnp.float32
BF16 = jnp.bfloat16

VMEM = pl.BlockSpec(memory_space=pltpu.VMEM)
SMEM = pl.BlockSpec(memory_space=pltpu.SMEM)


def call(body, outs, ins, scratch=(), flops=0, traffic=0):
    specs = [SMEM if a.dtype == jnp.int32 else VMEM for a in ins]
    return pl.pallas_call(
        body,
        out_shape=[jax.ShapeDtypeStruct(s, t) for s, t in outs],
        in_specs=specs,
        out_specs=[VMEM] * len(outs),
        scratch_shapes=list(scratch),
        compiler_params=pltpu.CompilerParams(vmem_limit_bytes=56 << 20),
        cost_estimate=pl.CostEstimate(flops=flops, bytes_accessed=traffic, transcendentals=0),
    )(*ins)


def chunks(total, step, body):
    whole = total // step

    def one(i, _):
        body(pl.multiple_of(i * step, step), step)
        return 0

    lax.fori_loop(0, whole, one, 0)
    if total % step:
        body(whole * step, total % step)


def cell(code):
    return code >> 6, code & 63


def spread(tab, blocks, sums, spread_ref):
    reach, depth = sums[0].shape[0], sums[0].shape[1]
    offsets = spread_ref.shape[0] // depth
    entries = tab.shape[0] // offsets
    ways = len(sums)

    def some(i, _):
        for acc in sums:
            acc[...] = jnp.zeros_like(acc)
        for e in range(entries):
            for w, acc in enumerate(sums):
                s, t = cell(tab[(i * ways + w) * entries + e])
                acc[s] = acc[s] + blocks[t]
        for w, acc in enumerate(sums):
            rows = pl.ds(pl.multiple_of((i * ways + w) * depth, depth), depth)
            for s in range(reach):
                spread_ref[rows, s * BLK : (s + 1) * BLK] = acc[s].astype(BF16)
        return 0

    lax.fori_loop(0, offsets // ways, some, 0)


def collect(tab, prod, sums, low, high):
    depth = sums[0].shape[1]
    offsets = prod.shape[0] // depth
    entries = tab.shape[0] // offsets
    idle = sums[0].shape[0] - 1
    for acc in sums:
        acc[...] = jnp.zeros_like(acc)

    def some(k, _):
        rows = pl.ds(pl.multiple_of(k * depth, depth), depth)
        for e in range(entries):
            acc = sums[e % len(sums)]
            s, t = cell(tab[k * entries + e])
            inside = (s >= low) & (s < high)
            t = jnp.where(inside, t, idle)
            s = jnp.where(inside, s - low, 0)
            acc[t] = acc[t] + prod[rows, pl.ds(pl.multiple_of(s * BLK, BLK), BLK)]
        return 0

    lax.fori_loop(0, offsets, some, 0)


def input_grad_body(nblocks, tab, info, cot_ref, w_ref, spread_ref, keep_ref, send_ref, blocks, part, *sums):
    depth = cot_ref.shape[0]
    for b in range(nblocks):
        blocks[b] = cot_ref[:, b * BLK : (b + 1) * BLK].astype(F32)
    blocks[nblocks] = jnp.zeros_like(blocks[nblocks])
    spread(tab, blocks, sums, spread_ref)

    def product(start, width):
        cols = pl.ds(start, width)
        res = lax.dot_general(w_ref[...], spread_ref[:, cols], (((0,), (0,)), ((), ())), preferred_element_type=F32)
        part[:, :, cols] = res.astype(BF16).reshape(part.shape[0], depth, width)

    chunks(spread_ref.shape[1], 2 * STEP, product)
    core = info[0]
    for j in range(keep_ref.shape[0]):
        keep_ref[j] = part[2 * j + core]
        send_ref[j] = part[2 * j + 1 - core]


def join_body(pieces, info, *refs):
    wide_ref, first_ref, last_ref = refs[pieces:]
    depth = refs[0].shape[0]
    for i, ref in enumerate(refs[:pieces]):
        place = info[8 + i]
        wide_ref[pl.ds(pl.multiple_of(place * depth, depth), depth), :] = ref[...]
    first_ref[...] = wide_ref[:, :RIM]
    start = pl.multiple_of((info[2] - HB) * BLK, BLK)
    last_ref[...] = wide_ref[:, pl.ds(start, RIM)]


def conv_inner_body(tab, w_ref, wide_ref, z_ref, prod, *sums):
    def product(start, width):
        cols = pl.ds(start, width)
        prod[:, cols] = jnp.dot(w_ref[...], wide_ref[:, cols], preferred_element_type=F32)

    nblocks = z_ref.shape[0]
    chunks(wide_ref.shape[1], STEP, product)
    collect(tab, prod, sums, 0, nblocks)
    for b in range(nblocks):
        total = sums[0][b]
        for acc in sums[1:]:
            total = total + acc[b]
        z_ref[b] = total


def conv_rim_body(layer, tab, w_ref, left_ref, right_ref, part_ref, *refs):
    outs, prod, sums = refs[: 2 if layer == 1 else 1], refs[2 if layer == 1 else 1], refs[3 if layer == 1 else 2 :]
    nblocks = part_ref.shape[0]
    prod[:, :RIM] = jnp.dot(w_ref[...], left_ref[...], preferred_element_type=F32)
    prod[:, RIM:] = jnp.dot(w_ref[...], right_ref[...], preferred_element_type=F32)
    collect(tab, prod, sums, nblocks, nblocks + 2 * HB)
    for b in range(nblocks):
        z = part_ref[b]
        for acc in sums:
            z = z + acc[b]
        cols = slice(b * BLK, (b + 1) * BLK)
        if layer == 1:
            outs[0][:, cols] = z
            outs[1][:, cols] = (z / (1.0 + jnp.exp(-z))).astype(BF16)
        else:
            outs[0][:, cols] = z.astype(BF16)


def halve_body(info, keep_ref, got_ref, mine_ref, *send_refs):
    place = info[1]
    mine_ref[...] = keep_ref[place].astype(F32) + got_ref[place].astype(F32)
    for j, ref in enumerate(send_refs):
        other = place ^ (j + 1)
        ref[...] = (keep_ref[other].astype(F32) + got_ref[other].astype(F32)).astype(BF16)


def rims_body(count, mine_ref, *refs):
    gots, (inner_ref, left_ref, right_ref) = refs[:count], refs[count:]
    total = mine_ref[...]
    for ref in gots:
        total = total + ref[...].astype(F32)
    rows = inner_ref.shape[1]
    inner_ref[...] = total[:, :rows]
    left_ref[...] = total[:, rows : rows + RIM].astype(BF16)
    right_ref[...] = total[:, rows + RIM :].astype(BF16)


def weight_grad(wide_ref, left_ref, right_ref, spread_ref, total, keep_ref, send_ref, parity):
    rows = wide_ref.shape[1]
    shares, width_in = total.shape[0], total.shape[1]
    dims = (((1,), (1,)), ((), ()))

    def product(start, width):
        part = pl.ds(start, width)
        res = lax.dot_general(wide_ref[...], spread_ref[part, :rows], dims, preferred_element_type=F32)
        res += lax.dot_general(left_ref[...], spread_ref[part, rows : rows + RIM], dims, preferred_element_type=F32)
        res += lax.dot_general(right_ref[...], spread_ref[part, rows + RIM :], dims, preferred_element_type=F32)
        total[:, :, part] = res.reshape(shares, width_in, width)

    chunks(spread_ref.shape[0], STEP, product)
    for j in range(shares // 2):
        keep_ref[j] = total[2 * j + parity]
        send_ref[j] = total[2 * j + 1 - parity].astype(BF16)


def grad_two_body(info, wide_ref, left_ref, right_ref, spread_ref, keep_ref, send_ref, total):
    weight_grad(wide_ref, left_ref, right_ref, spread_ref, total, keep_ref, send_ref, info[3])


def grad_one_body(
    tab, info, z_ref, inner_ref, from_left, from_right, wide_ref, left_ref, right_ref,
    keep_ref, send_ref, grads, blocks, spread_ref, total, *sums
):
    grads[...] = inner_ref[...]
    grads[:, :RIM] = grads[:, :RIM] + from_left[...].astype(F32)
    tail = pl.ds(pl.multiple_of((info[2] - HB) * BLK, BLK), RIM)
    grads[:, tail] = grads[:, tail] + from_right[...].astype(F32)
    nblocks = blocks.shape[0] - 1
    for b in range(nblocks):
        cols = slice(b * BLK, (b + 1) * BLK)
        z = z_ref[:, cols]
        gate = 1.0 / (1.0 + jnp.exp(-z))
        value = grads[:, cols] * gate * (1.0 + z * (1.0 - gate))
        blocks[b] = value.astype(BF16).astype(F32)
    blocks[nblocks] = jnp.zeros_like(blocks[nblocks])
    spread(tab, blocks, sums, spread_ref)
    weight_grad(wide_ref, left_ref, right_ref, spread_ref, total, keep_ref, send_ref, info[3])


def finish_body(count, mine_ref, *refs):
    gots, out_ref = refs[:count], refs[count]
    total = mine_ref[...]
    for ref in gots:
        total = total + ref[...].astype(F32)
    depth = out_ref.shape[2]
    for k in range(out_ref.shape[0]):
        out_ref[k] = total[:, k * depth : (k + 1) * depth]


def local(features, kernel_map, block_count, weight_one, weight_two, cotangent):
    shard, place = lax.axis_index("space"), lax.axis_index("chan")
    slabs, parts = lax.axis_size("space"), lax.axis_size("chan")
    pairs = parts // 2
    rows, depth = features.shape
    nblocks = rows // BLK
    reach = nblocks + 2 * HB
    offsets, entries = kernel_map.shape[1:3]
    wide = weight_one.shape[2]
    flat = offsets * depth

    own_count = block_count[shard]
    left_count = block_count[jnp.maximum(shard - 1, 0)]
    source, inblock, target = (kernel_map[0, :, :, i] for i in range(3))
    position = jnp.where(
        source == shard,
        inblock,
        jnp.where(source < shard, nblocks + inblock - (left_count - HB), nblocks + HB + inblock),
    )
    tab = (position * 64 + jnp.where(target < own_count, target, nblocks)).reshape(-1)
    order = [0, 1] + [v for j in range(1, pairs) for v in (2 * j, 2 * j + 1)]
    info = jnp.stack(
        [place % 2, place // 2, own_count, shard % 2, shard // 2, shard * 0, shard * 0, shard * 0]
        + [place ^ v for v in order]
    ).astype(jnp.int32)

    def swap(value, axis, bits):
        return lax.ppermute(value, axis, [(i, i ^ bits) for i in range(lax.axis_size(axis))])

    def up(value):
        return lax.ppermute(value, "space", [(i, i + 1) for i in range(slabs - 1)])

    def down(value):
        return lax.ppermute(value, "space", [(i + 1, i) for i in range(slabs - 1)])

    def gather(shard_t):
        pieces = [shard_t]
        far = [swap(shard_t, "chan", 2 * j) for j in range(1, pairs)]
        pieces.append(swap(shard_t, "chan", 1))
        for got in far:
            pieces += [got, swap(got, "chan", 1)]
        joined, first, last = call(
            functools.partial(join_body, parts),
            [((wide, rows), BF16), ((wide, RIM), BF16), ((wide, RIM), BF16)],
            [info] + pieces,
            traffic=4 << 20,
        )
        return joined, up(last), down(first)

    sum_block = pltpu.VMEM((nblocks + 1, depth, BLK), F32)
    reach_block = pltpu.VMEM((reach, depth, BLK), F32)

    def conv_inner(weights, joined):
        return call(
            conv_inner_body,
            [((nblocks, depth, BLK), F32)],
            [tab, weights, joined],
            [pltpu.VMEM((flat, rows), F32)] + [sum_block] * 4,
            flops=2 * flat * wide * rows,
            traffic=16 << 20,
        )[0]

    def conv_rim(layer, weights, left, right, part):
        return call(
            functools.partial(conv_rim_body, layer),
            [((depth, rows), F32), ((depth, rows), BF16)] if layer == 1 else [((depth, rows), BF16)],
            [tab, weights, left, right, part],
            [pltpu.VMEM((flat, 2 * RIM), F32)] + [sum_block] * 4,
            flops=2 * flat * wide * 2 * RIM,
            traffic=8 << 20,
        )

    def reduce_slabs(keep, send):
        got = swap(send, "space", 1)
        share = wide // slabs
        outs = call(
            halve_body,
            [((share, flat), F32)] + [((share, flat), BF16)] * (slabs // 2 - 1),
            [info_z, keep, got],
            traffic=4 << 20,
        )
        gots = [swap(v, "space", 2 * (j + 1)) for j, v in enumerate(outs[1:])]
        total = call(
            functools.partial(finish_body, len(gots)),
            [((offsets, share, depth), F32)],
            [outs[0]] + gots,
            traffic=2 << 20,
        )[0]
        return total.transpose(0, 2, 1)

    info_z = jnp.stack([shard % 2, shard // 2]).astype(jnp.int32)
    w_one = weight_one.reshape(flat, wide)
    w_two = weight_two.reshape(flat, wide)

    x_wide, x_left, x_right = gather(features.T)

    spread_two, keep, send = call(
        functools.partial(input_grad_body, nblocks),
        [((flat, reach * BLK), BF16), ((pairs, depth, reach * BLK), BF16), ((pairs, depth, reach * BLK), BF16)],
        [tab, info, cotangent.T, w_two],
        [pltpu.VMEM((nblocks + 1, depth, BLK), F32), pltpu.VMEM((parts, depth, reach * BLK), BF16)] + [reach_block] * 3,
        flops=2 * flat * wide * reach * BLK,
        traffic=24 << 20,
    )
    got = swap(send, "chan", 1)
    mine, *sends = call(
        halve_body,
        [((depth, reach * BLK), F32)] + [((depth, reach * BLK), BF16)] * (pairs - 1),
        [info, keep, got],
        traffic=4 << 20,
    )
    gots = [swap(v, "chan", 2 * (j + 1)) for j, v in enumerate(sends)]

    z_part = conv_inner(w_one, x_wide)
    z_one, hidden = conv_rim(1, w_one, x_left, x_right, z_part)
    h_wide, h_left, h_right = gather(hidden)

    inner, to_left, to_right = call(
        functools.partial(rims_body, len(gots)),
        [((depth, rows), F32), ((depth, RIM), BF16), ((depth, RIM), BF16)],
        [mine] + gots,
        traffic=3 << 20,
    )
    from_right, from_left = down(to_left), up(to_right)

    share = wide // slabs
    grad_outs = [((slabs // 2, share, flat), F32), ((slabs // 2, share, flat), BF16)]
    total_scratch = pltpu.VMEM((slabs, share, flat), F32)
    keep_one, send_one = call(
        grad_one_body,
        grad_outs,
        [tab, info, z_one, inner, from_left, from_right, x_wide, x_left, x_right],
        [
            pltpu.VMEM((depth, rows), F32),
            pltpu.VMEM((nblocks + 1, depth, BLK), F32),
            pltpu.VMEM((flat, reach * BLK), BF16),
            total_scratch,
        ]
        + [reach_block] * 3,
        flops=2 * flat * wide * reach * BLK,
        traffic=24 << 20,
    )
    grad_one = reduce_slabs(keep_one, send_one)

    out_part = conv_inner(w_two, h_wide)
    keep_two, send_two = call(
        grad_two_body,
        grad_outs,
        [info, h_wide, h_left, h_right, spread_two],
        [total_scratch],
        flops=2 * flat * wide * reach * BLK,
        traffic=16 << 20,
    )
    grad_two = reduce_slabs(keep_two, send_two)
    (output,) = conv_rim(2, w_two, h_left, h_right, out_part)
    return output.T, grad_one, grad_two


def solution(mesh):
    return jax.shard_map(
        local,
        mesh=mesh,
        in_specs=(
            P("space", "chan"),
            P("space", None, None, None),
            P(),
            P(None, "chan", None),
            P(None, "chan", None),
            P("space", "chan"),
        ),
        out_specs=(P("space", "chan"), P(None, "chan", "space"), P(None, "chan", "space")),
        check_vma=False,
    )
```

```python
import functools

import jax
import jax.numpy as jnp
from jax import lax
from jax.experimental import pallas as pl
from jax.experimental.pallas import tpu as pltpu
from jax.sharding import PartitionSpec as P

BLK = 128
HB = 2
RIM = HB * BLK
STEP = 256
F32 = jnp.float32
BF16 = jnp.bfloat16

VMEM = pl.BlockSpec(memory_space=pltpu.VMEM)
SMEM = pl.BlockSpec(memory_space=pltpu.SMEM)


def held(value):
    return pltpu.with_memory_space_constraint(value, pltpu.VMEM)


def call(body, outs, ins, scratch=(), flops=0, traffic=0, vmem=40):
    specs = [SMEM if a.dtype == jnp.int32 and a.ndim < 3 else VMEM for a in ins]
    return pl.pallas_call(
        body,
        out_shape=outs,
        in_specs=specs,
        out_specs=[VMEM] * len(outs),
        scratch_shapes=list(scratch),
        compiler_params=pltpu.CompilerParams(vmem_limit_bytes=vmem << 20),
        cost_estimate=pl.CostEstimate(flops=flops, bytes_accessed=traffic, transcendentals=0),
    )(*ins)


def chunks(total, step, body):
    whole = total // step

    def one(i, _):
        body(pl.multiple_of(i * step, step), step)
        return 0

    lax.fori_loop(0, whole, one, 0)
    if total % step:
        body(whole * step, total % step)


def cell(code):
    return code >> 6, code & 63


def near_rim(counts):
    shard = lax.axis_index("space")
    tail = (counts[shard] - HB) * BLK
    even = shard % 2 == 0
    return pl.multiple_of(jnp.where(even, tail, 0), BLK), pl.multiple_of(jnp.where(even, 0, tail), BLK)


def table(counts, map_ref, nblocks):
    shard = lax.axis_index("space")
    even = shard % 2 == 0
    own_count, left_count = counts[shard], counts[jnp.maximum(shard - 1, 0)]
    source, inblock, target = map_ref[0], map_ref[1], map_ref[2]
    left = jnp.where(even, nblocks + HB, nblocks) - (left_count - HB)
    right = jnp.where(even, nblocks, nblocks + HB)
    position = inblock + jnp.where(source == shard, 0, jnp.where(source < shard, left, right))
    code = position * 64 + jnp.where(target < own_count, target, nblocks)
    entries = code.shape[0]
    index = lax.broadcasted_iota(jnp.int32, code.shape, 0)
    rank = jnp.zeros_like(code)
    for e in range(entries):
        row = code[e : e + 1]
        rank += ((row < code) | ((row == code) & (e < index))).astype(jnp.int32)
    rows = [jnp.sum(jnp.where(rank == e, code, 0), axis=0, keepdims=True) for e in range(entries)]
    return jnp.concatenate(rows, axis=0)


def spread(tab, blocks, spread_ref):
    depth = blocks.shape[1]
    entries, offsets = tab.shape

    def one(k, _):
        rows = pl.ds(pl.multiple_of(k * depth, depth), depth)
        spread_ref[rows, :] = jnp.zeros((depth, spread_ref.shape[1]), BF16)
        before, acc = -1, jnp.zeros((depth, BLK), F32)
        for e in range(entries):
            s, t = cell(tab[e, k])
            acc = jnp.where(s == before, acc, 0.0) + blocks[t]
            spread_ref[rows, pl.ds(pl.multiple_of(s * BLK, BLK), BLK)] = acc.astype(BF16)
            before = s
        return 0

    lax.fori_loop(0, offsets, one, 0)


def collect(tab, prod, sums):
    depth = sums[0].shape[1]
    entries, offsets = tab.shape
    for acc in sums:
        acc[...] = jnp.zeros_like(acc)

    def one(k, _):
        rows = pl.ds(pl.multiple_of(k * depth, depth), depth)
        for e in range(entries):
            acc = sums[e % len(sums)]
            s, t = cell(tab[e, k])
            acc[t] = acc[t] + prod[rows, pl.ds(pl.multiple_of(s * BLK, BLK), BLK)]
        return 0

    lax.fori_loop(0, offsets, one, 0)


def extend(ext_ref, wide_ref, a_ref, b_ref):
    rows = wide_ref.shape[1]
    ext_ref[:, :rows] = wide_ref[...]
    ext_ref[:, rows : rows + RIM] = a_ref[...]
    ext_ref[:, rows + RIM :] = b_ref[...]


def input_grad_body(counts, map_ref, cot_ref, w_ref, tab_ref, spread_ref, keep_ref, send_ref, blocks, part, tab, sem):
    depth, rows = cot_ref.shape
    nblocks = rows // BLK
    tab_ref[...] = table(counts, map_ref, nblocks)
    copy = pltpu.make_async_copy(tab_ref, tab, sem)
    copy.start()
    for b in range(nblocks):
        blocks[b] = cot_ref[:, b * BLK : (b + 1) * BLK].astype(F32)
    blocks[nblocks] = jnp.zeros_like(blocks[nblocks])
    copy.wait()
    spread(tab, blocks, spread_ref)

    def product(start, width):
        cols = pl.ds(start, width)
        res = lax.dot_general(w_ref[...], spread_ref[:, cols], (((0,), (0,)), ((), ())), preferred_element_type=F32)
        part[:, :, cols] = res.astype(BF16).reshape(part.shape[0], depth, width)

    chunks(spread_ref.shape[1], 2 * STEP, product)
    core = lax.axis_index("chan") % 2
    for j in range(keep_ref.shape[0]):
        keep_ref[j] = part[2 * j + core]
        send_ref[j] = part[2 * j + 1 - core]


def join_body(order, counts, *refs):
    pieces = len(order)
    wide_ref, a_ref, b_ref = refs[pieces:]
    depth = refs[0].shape[0]
    for bits, ref in zip(order, refs[:pieces]):
        place = lax.axis_index("chan") ^ bits
        wide_ref[pl.ds(pl.multiple_of(place * depth, depth), depth), :] = ref[...]
    a, b = near_rim(counts)
    a_ref[...] = wide_ref[:, pl.ds(a, RIM)]
    b_ref[...] = wide_ref[:, pl.ds(b, RIM)]


def conv_body(layer, tab, w_ref, wide_ref, a_ref, b_ref, *refs):
    count = 2 if layer == 1 else 1
    outs, ext, prod, sums = refs[:count], refs[count], refs[count + 1], refs[count + 2 :]
    extend(ext, wide_ref, a_ref, b_ref)

    def product(start, width):
        cols = pl.ds(start, width)
        prod[:, cols] = jnp.dot(w_ref[...], ext[:, cols], preferred_element_type=F32)

    chunks(ext.shape[1], 2 * STEP, product)
    collect(tab, prod, sums)
    for b in range(sums[0].shape[0] - 1):
        z = sums[0][b]
        for acc in sums[1:]:
            z = z + acc[b]
        cols = slice(b * BLK, (b + 1) * BLK)
        if layer == 1:
            outs[0][:, cols] = z
            outs[1][:, cols] = (z / (1.0 + jnp.exp(-z))).astype(BF16)
        else:
            outs[0][:, cols] = z.astype(BF16)


def halve_body(axis, keep_ref, got_ref, mine_ref, *send_refs):
    place = lax.axis_index(axis) // 2
    mine_ref[...] = keep_ref[place].astype(F32) + got_ref[place].astype(F32)
    for j, ref in enumerate(send_refs):
        other = place ^ (j + 1)
        ref[...] = (keep_ref[other].astype(F32) + got_ref[other].astype(F32)).astype(BF16)


def rims_body(count, mine_ref, *refs):
    gots, (inner_ref, a_ref, b_ref) = refs[:count], refs[count:]
    total = mine_ref[...]
    for ref in gots:
        total = total + ref[...].astype(F32)
    rows = inner_ref.shape[1]
    inner_ref[...] = total[:, :rows]
    a_ref[...] = total[:, rows : rows + RIM].astype(BF16)
    b_ref[...] = total[:, rows + RIM :].astype(BF16)


def weight_grad(ext, spread_ref, total, keep_ref, send_ref):
    shares, width_in = total.shape[0], total.shape[1]

    def product(start, width):
        part = pl.ds(start, width)
        res = lax.dot_general(ext[...], spread_ref[part, :], (((1,), (1,)), ((), ())), preferred_element_type=F32)
        total[:, :, part] = res.reshape(shares, width_in, width)

    chunks(spread_ref.shape[0], 2 * STEP, product)
    parity = lax.axis_index("space") % 2
    for j in range(shares // 2):
        keep_ref[j] = total[2 * j + parity]
        send_ref[j] = total[2 * j + 1 - parity].astype(BF16)


def grad_two_body(wide_ref, a_ref, b_ref, spread_ref, keep_ref, send_ref, ext, total):
    extend(ext, wide_ref, a_ref, b_ref)
    weight_grad(ext, spread_ref, total, keep_ref, send_ref)


def grad_one_body(
    counts, tab, z_ref, inner_ref, from_a, from_b, wide_ref, a_ref, b_ref,
    keep_ref, send_ref, grads, blocks, spread_ref, ext, total
):
    extend(ext, wide_ref, a_ref, b_ref)
    grads[...] = inner_ref[...]
    a, b = near_rim(counts)
    for start, ref in ((a, from_a), (b, from_b)):
        grads[:, pl.ds(start, RIM)] = grads[:, pl.ds(start, RIM)] + ref[...].astype(F32)
    nblocks = blocks.shape[0] - 1
    for i in range(nblocks):
        cols = slice(i * BLK, (i + 1) * BLK)
        z = z_ref[:, cols]
        gate = 1.0 / (1.0 + jnp.exp(-z))
        value = grads[:, cols] * gate * (1.0 + z * (1.0 - gate))
        blocks[i] = value.astype(BF16).astype(F32)
    blocks[nblocks] = jnp.zeros_like(blocks[nblocks])
    spread(tab, blocks, spread_ref)
    weight_grad(ext, spread_ref, total, keep_ref, send_ref)


def finish_body(count, mine_ref, *refs):
    gots, out_ref = refs[:count], refs[count]
    total = mine_ref[...]
    for ref in gots:
        total = total + ref[...].astype(F32)
    depth = out_ref.shape[2]
    for k in range(out_ref.shape[0]):
        out_ref[k] = total[:, k * depth : (k + 1) * depth]


def swap(value, axis, bits):
    return lax.ppermute(value, axis, [(i, i ^ bits) for i in range(lax.axis_size(axis))])


def swap_other(value):
    pairs = [(i, i + 1) for i in range(1, lax.axis_size("space") - 1, 2)]
    return lax.ppermute(value, "space", pairs + [(j, i) for i, j in pairs])


def local(features, kernel_map, block_count, weight_one, weight_two, cotangent):
    slabs, parts = lax.axis_size("space"), lax.axis_size("chan")
    pairs = parts // 2
    rows, depth = features.shape
    nblocks = rows // BLK
    reach = (nblocks + 2 * HB) * BLK
    offsets, entries = kernel_map.shape[1:3]
    wide = weight_one.shape[2]
    flat = offsets * depth
    share = wide // slabs
    order = [0, 1] + [v for j in range(1, pairs) for v in (2 * j, 2 * j + 1)]
    work = 2 * flat * wide * reach
    blocks = pltpu.VMEM((nblocks + 1, depth, BLK), F32)
    ext = pltpu.VMEM((wide, reach), BF16)

    def gather(shard_t):
        far = [swap(shard_t, "chan", 2 * j) for j in range(1, pairs)]
        pieces = [shard_t, swap(shard_t, "chan", 1)]
        for got in far:
            pieces += [got, swap(got, "chan", 1)]
        joined, a, b = call(
            functools.partial(join_body, order),
            [pltpu.VMEM((wide, rows), BF16), pltpu.VMEM((wide, RIM), BF16), pltpu.VMEM((wide, RIM), BF16)],
            [block_count] + [held(v) for v in pieces],
            traffic=2 << 20,
        )
        return joined, swap(a, "space", 1), swap_other(b)

    def convolve(layer, weights, joined, a, b):
        out = pltpu.VMEM((depth, rows), BF16)
        return call(
            functools.partial(conv_body, layer),
            [pltpu.VMEM((depth, rows), F32), out] if layer == 1 else [jax.ShapeDtypeStruct((depth, rows), BF16)],
            [tab, weights, held(joined), held(a), held(b)],
            [ext, pltpu.VMEM((flat, reach), F32)] + [blocks] * 2,
            flops=work,
            traffic=16 << 20,
        )

    def reduce_slabs(keep, send):
        got = swap(send, "space", 1)
        outs = call(
            functools.partial(halve_body, "space"),
            [pltpu.VMEM((share, flat), F32)] + [pltpu.VMEM((share, flat), BF16)] * (slabs // 2 - 1),
            [held(keep), held(got)],
            traffic=2 << 20,
        )
        gots = [swap(v, "space", 2 * (j + 1)) for j, v in enumerate(outs[1:])]
        total = call(
            functools.partial(finish_body, len(gots)),
            [jax.ShapeDtypeStruct((offsets, share, depth), F32)],
            [held(v) for v in [outs[0]] + gots],
            traffic=2 << 20,
        )[0]
        return total.transpose(0, 2, 1)

    w_one = weight_one.reshape(flat, wide)
    w_two = weight_two.reshape(flat, wide)

    x_wide, x_a, x_b = gather(features.T)

    tab, spread_two, keep, send = call(
        input_grad_body,
        [
            jax.ShapeDtypeStruct((entries, offsets), jnp.int32),
            pltpu.VMEM((flat, reach), BF16),
            pltpu.VMEM((pairs, depth, reach), BF16),
            pltpu.VMEM((pairs, depth, reach), BF16),
        ],
        [block_count, kernel_map[0].transpose(2, 1, 0), cotangent.T, w_two],
        [
            blocks,
            pltpu.VMEM((parts, depth, reach), BF16),
            pltpu.SMEM((entries, offsets), jnp.int32),
            pltpu.SemaphoreType.DMA,
        ],
        flops=work,
        traffic=16 << 20,
    )
    got = swap(send, "chan", 1)
    mine, *sends = call(
        functools.partial(halve_body, "chan"),
        [pltpu.VMEM((depth, reach), F32)] + [pltpu.VMEM((depth, reach), BF16)] * (pairs - 1),
        [held(keep), held(got)],
        traffic=2 << 20,
    )
    gots = [swap(v, "chan", 2 * (j + 1)) for j, v in enumerate(sends)]

    z_one, hidden = convolve(1, w_one, x_wide, x_a, x_b)
    h_wide, h_a, h_b = gather(hidden)

    inner, to_a, to_b = call(
        functools.partial(rims_body, len(gots)),
        [pltpu.VMEM((depth, rows), F32), pltpu.VMEM((depth, RIM), BF16), pltpu.VMEM((depth, RIM), BF16)],
        [held(v) for v in [mine] + gots],
        traffic=2 << 20,
    )
    from_a, from_b = swap(to_a, "space", 1), swap_other(to_b)

    grad_outs = [pltpu.VMEM((slabs // 2, share, flat), F32), pltpu.VMEM((slabs // 2, share, flat), BF16)]
    total_scratch = pltpu.VMEM((slabs, share, flat), F32)
    keep_one, send_one = call(
        grad_one_body,
        grad_outs,
        [block_count, tab] + [held(v) for v in (z_one, inner, from_a, from_b, x_wide, x_a, x_b)],
        [pltpu.VMEM((depth, rows), F32), blocks, pltpu.VMEM((flat, reach), BF16), ext, total_scratch],
        flops=work,
        traffic=16 << 20,
    )
    grad_one = reduce_slabs(keep_one, send_one)

    keep_two, send_two = call(
        grad_two_body,
        grad_outs,
        [held(v) for v in (h_wide, h_a, h_b, spread_two)],
        [ext, total_scratch],
        flops=work,
        traffic=8 << 20,
    )
    grad_two = reduce_slabs(keep_two, send_two)
    (output,) = convolve(2, w_two, h_wide, h_a, h_b)
    return output.T, grad_one, grad_two


def solution(mesh):
    return jax.shard_map(
        local,
        mesh=mesh,
        in_specs=(
            P("space", "chan"),
            P("space", None, None, None),
            P(),
            P(None, "chan", None),
            P(None, "chan", None),
            P("space", "chan"),
        ),
        out_specs=(P("space", "chan"), P(None, "chan", "space"), P(None, "chan", "space")),
        check_vma=False,
    )
```

```python
import functools

import jax
import jax.numpy as jnp
from jax import lax
from jax.experimental import pallas as pl
from jax.experimental.pallas import tpu as pltpu
from jax.sharding import PartitionSpec as P

BLK = 128
HB = 2
RIM = HB * BLK
STEP = 256
F32 = jnp.float32
BF16 = jnp.bfloat16

VMEM = pl.BlockSpec(memory_space=pltpu.VMEM)
SMEM = pl.BlockSpec(memory_space=pltpu.SMEM)
FAR = pl.BlockSpec(memory_space=pltpu.HBM)
PAD = 8


def held(value):
    return pltpu.with_memory_space_constraint(value, pltpu.VMEM)


def call(body, outs, ins, scratch=(), flops=0, traffic=0, vmem=6, specs=None, after=(), aliases=None):
    specs = list(specs or [SMEM if a.dtype == jnp.int32 else VMEM for a in ins])
    first, last = len(ins), len(ins) + len(after)
    ins = list(ins) + [held(v) for v in after]
    specs += [VMEM] * len(after)

    def ordered(*refs):
        body(*refs[:first], *refs[last:])

    return pl.pallas_call(
        ordered,
        out_shape=outs,
        in_specs=specs,
        out_specs=[VMEM] * len(outs),
        scratch_shapes=list(scratch),
        input_output_aliases=aliases or {},
        compiler_params=pltpu.CompilerParams(vmem_limit_bytes=vmem << 20),
        cost_estimate=pl.CostEstimate(flops=flops, bytes_accessed=traffic, transcendentals=0),
    )(*ins)


def chunks(total, step, body):
    whole = total // step

    def one(i, _):
        body(pl.multiple_of(i * step, step), step)
        return 0

    lax.fori_loop(0, whole, one, 0)
    if total % step:
        body(whole * step, total % step)


def cell(code):
    return code >> 6, code & 63


def near_rim(tab):
    row = tab.shape[0] - PAD
    return pl.multiple_of(tab[row, 0], BLK), pl.multiple_of(tab[row, 1], BLK)


def table(counts, map_ref, nblocks):
    shard = lax.axis_index("space")
    even = shard % 2 == 0
    own_count, left_count = counts[shard], counts[jnp.maximum(shard - 1, 0)]
    source, inblock, target = map_ref[0], map_ref[1], map_ref[2]
    left = jnp.where(even, nblocks + HB, nblocks) - (left_count - HB)
    right = jnp.where(even, nblocks, nblocks + HB)
    position = inblock + jnp.where(source == shard, 0, jnp.where(source < shard, left, right))
    code = position * 64 + jnp.where(target < own_count, target, nblocks)
    entries = code.shape[0]
    index = lax.broadcasted_iota(jnp.int32, code.shape, 0)
    rank = jnp.zeros_like(code)
    for e in range(entries):
        row = code[e : e + 1]
        rank += ((row < code) | ((row == code) & (e < index))).astype(jnp.int32)
    rows = [jnp.sum(jnp.where(rank == e, code, 0), axis=0, keepdims=True) for e in range(entries)]
    tail = (own_count - HB) * BLK
    spot = (lax.broadcasted_iota(jnp.int32, (PAD, code.shape[1]), 1) == 0) == even
    return jnp.concatenate(rows + [jnp.where(spot, tail, 0)], axis=0)


def spread(tab, blocks, spread_ref):
    depth = blocks.shape[1]
    entries, offsets = tab.shape[0] - PAD, tab.shape[1]

    def one(k, _):
        rows = pl.ds(pl.multiple_of(k * depth, depth), depth)
        spread_ref[rows, :] = jnp.zeros((depth, spread_ref.shape[1]), BF16)
        before, acc = -1, jnp.zeros((depth, BLK), F32)
        for e in range(entries):
            s, t = cell(tab[e, k])
            acc = jnp.where(s == before, acc, 0.0) + blocks[t]
            spread_ref[rows, pl.ds(pl.multiple_of(s * BLK, BLK), BLK)] = acc.astype(BF16)
            before = s
        return 0

    lax.fori_loop(0, offsets, one, 0)


def collect(tab, prod, sums):
    depth = sums[0].shape[1]
    entries, offsets = tab.shape[0] - PAD, tab.shape[1]
    for acc in sums:
        acc[...] = jnp.zeros_like(acc)

    def one(k, _):
        rows = pl.ds(pl.multiple_of(k * depth, depth), depth)
        for e in range(entries):
            acc = sums[e % len(sums)]
            s, t = cell(tab[e, k])
            acc[t] = acc[t] + prod[rows, pl.ds(pl.multiple_of(s * BLK, BLK), BLK)]
        return 0

    lax.fori_loop(0, offsets, one, 0)


def lay(ext_ref, order, refs):
    depth = refs[0].shape[0]
    for bits, ref in zip(order, refs):
        place = lax.axis_index("chan") ^ bits
        ext_ref[pl.ds(pl.multiple_of(place * depth, depth), depth), :] = ref[...]


def extend(ext_ref, wide_ref, a_ref, b_ref):
    rows = wide_ref.shape[1]
    ext_ref[:, :rows] = wide_ref[...]
    ext_ref[:, rows : rows + RIM] = a_ref[...]
    ext_ref[:, rows + RIM :] = b_ref[...]


def input_grad_body(
    counts, map_hbm, cot_hbm, w_hbm, tab_ref, spread_ref, keep_ref, send_ref,
    map_ref, cot_ref, w_ref, blocks, part, tab, sems, sem
):
    loads = [
        pltpu.make_async_copy(src, dst, sems.at[i])
        for i, (src, dst) in enumerate([(map_hbm, map_ref), (cot_hbm, cot_ref), (w_hbm, w_ref)])
    ]
    for load in loads:
        load.start()
    depth, rows = cot_ref.shape
    nblocks = rows // BLK
    loads[0].wait()
    tab_ref[...] = table(counts, map_ref, nblocks)
    copy = pltpu.make_async_copy(tab_ref, tab, sem)
    copy.start()
    loads[1].wait()
    for b in range(nblocks):
        blocks[b] = cot_ref[:, b * BLK : (b + 1) * BLK].astype(F32)
    blocks[nblocks] = jnp.zeros_like(blocks[nblocks])
    copy.wait()
    spread(tab, blocks, spread_ref)
    loads[2].wait()

    def product(start, width):
        cols = pl.ds(start, width)
        res = lax.dot_general(w_ref[...], spread_ref[:, cols], (((0,), (0,)), ((), ())), preferred_element_type=F32)
        part[:, :, cols] = res.astype(BF16).reshape(part.shape[0], depth, width)

    chunks(spread_ref.shape[1], 2 * STEP, product)
    core = lax.axis_index("chan") % 2
    for j in range(keep_ref.shape[0]):
        keep_ref[j] = part[2 * j + core]
        send_ref[j] = part[2 * j + 1 - core]


def pass_body(value_ref, out_ref):
    out_ref[...] = value_ref[...]


def join_body(order, tab, *refs):
    pieces = len(order)
    wide_ref, a_ref, b_ref = refs[pieces:]
    lay(wide_ref, order, refs[:pieces])
    a, b = near_rim(tab)
    a_ref[...] = wide_ref[:, pl.ds(a, RIM)]
    b_ref[...] = wide_ref[:, pl.ds(b, RIM)]


def multiply(w_ref, value_ref, prod):
    def product(start, width):
        cols = pl.ds(start, width)
        prod[:, cols] = jnp.dot(w_ref[...], value_ref[:, cols], preferred_element_type=F32)

    chunks(value_ref.shape[1], 2 * STEP, product)


def gather_sums(tab, prod, sums, store):
    collect(tab, prod, sums)
    for b in range(sums[0].shape[0] - 1):
        total = sums[0][b]
        for acc in sums[1:]:
            total = total + acc[b]
        store(slice(b * BLK, (b + 1) * BLK), total)


def inner_body(w_ref, wide_ref, prod_ref):
    multiply(w_ref, wide_ref, prod_ref)


def hidden_body(tab, w_ref, a_ref, b_ref, _, z_ref, hidden_ref, prod, *sums):
    rows = z_ref.shape[1]
    prod[:, rows : rows + RIM] = jnp.dot(w_ref[...], a_ref[...], preferred_element_type=F32)
    prod[:, rows + RIM :] = jnp.dot(w_ref[...], b_ref[...], preferred_element_type=F32)

    def store(cols, z):
        z_ref[:, cols] = z
        hidden_ref[:, cols] = (z / (1.0 + jnp.exp(-z))).astype(BF16)

    gather_sums(tab, prod, sums, store)


def output_body(order, tab, w_ref, *refs):
    pieces = len(order)
    out_ref, ext, prod, *sums = refs[pieces:]
    lay(ext, order, refs[:pieces])

    def store(cols, total):
        out_ref[:, cols] = total.astype(BF16)

    multiply(w_ref, ext, prod)
    gather_sums(tab, prod, sums, store)


def halve_body(axis, keep_ref, got_ref, mine_ref, *send_refs):
    place = lax.axis_index(axis) // 2
    mine_ref[...] = keep_ref[place].astype(F32) + got_ref[place].astype(F32)
    for j, ref in enumerate(send_refs):
        other = place ^ (j + 1)
        ref[...] = (keep_ref[other].astype(F32) + got_ref[other].astype(F32)).astype(BF16)


def turn_body(count, tab, hidden_ref, mine_ref, *refs):
    gots, (inner_ref, a_ref, b_ref) = refs[:count], refs[count:]
    total = mine_ref[...]
    for ref in gots:
        total = total + ref[...].astype(F32)
    rows = inner_ref.shape[1]
    inner_ref[...] = total[:, :rows]
    a, b = near_rim(tab)
    a_ref[0] = total[:, rows : rows + RIM].astype(BF16)
    a_ref[1] = hidden_ref[:, pl.ds(a, RIM)]
    b_ref[0] = total[:, rows + RIM :].astype(BF16)
    b_ref[1] = hidden_ref[:, pl.ds(b, RIM)]


def pack_body(hidden_ref, a_ref, b_ref, rim_ref, full_ref):
    rows = hidden_ref.shape[1]
    rim_ref[:, :RIM] = a_ref[1]
    rim_ref[:, RIM:] = b_ref[1]
    full_ref[:, :rows] = hidden_ref[...]
    full_ref[:, rows:] = rim_ref[...]


def append_body(wide_ref, rim_ref, full_ref):
    rows = wide_ref.shape[1]
    full_ref[:, :rows] = wide_ref[...]
    full_ref[:, rows:] = rim_ref[...]


def weight_grad(ext, spread_ref, total, keep_ref, send_ref):
    shares, width_in = total.shape[0], total.shape[1]

    def product(start, width):
        part = pl.ds(start, width)
        res = lax.dot_general(ext[...], spread_ref[part, :], (((1,), (1,)), ((), ())), preferred_element_type=F32)
        total[:, :, part] = res.reshape(shares, width_in, width)

    chunks(spread_ref.shape[0], 2 * STEP, product)
    parity = lax.axis_index("space") % 2
    for j in range(shares // 2):
        keep_ref[j] = total[2 * j + parity]
        send_ref[j] = total[2 * j + 1 - parity].astype(BF16)


def grad_two_body(order, spread_ref, *refs):
    pieces = len(order)
    keep_ref, send_ref, ext, total = refs[pieces:]
    lay(ext, order, refs[:pieces])
    weight_grad(ext, spread_ref, total, keep_ref, send_ref)


def grad_one_body(
    tab, z_ref, inner_ref, from_a, from_b, wide_ref, a_ref, b_ref,
    keep_ref, send_ref, grads, blocks, spread_ref, ext, total
):
    extend(ext, wide_ref, a_ref, b_ref)
    grads[...] = inner_ref[...]
    a, b = near_rim(tab)
    for start, ref in ((a, from_a), (b, from_b)):
        grads[:, pl.ds(start, RIM)] = grads[:, pl.ds(start, RIM)] + ref[0].astype(F32)
    nblocks = blocks.shape[0] - 1
    for i in range(nblocks):
        cols = slice(i * BLK, (i + 1) * BLK)
        z = z_ref[:, cols]
        gate = 1.0 / (1.0 + jnp.exp(-z))
        value = grads[:, cols] * gate * (1.0 + z * (1.0 - gate))
        blocks[i] = value.astype(BF16).astype(F32)
    blocks[nblocks] = jnp.zeros_like(blocks[nblocks])
    spread(tab, blocks, spread_ref)
    weight_grad(ext, spread_ref, total, keep_ref, send_ref)


def finish_body(count, mine_ref, *refs):
    gots, out_ref = refs[:count], refs[count]
    total = mine_ref[...]
    for ref in gots:
        total = total + ref[...].astype(F32)
    depth = out_ref.shape[2]
    for k in range(out_ref.shape[0]):
        out_ref[k] = total[:, k * depth : (k + 1) * depth]


def swap(value, axis, bits):
    return lax.ppermute(value, axis, [(i, i ^ bits) for i in range(lax.axis_size(axis))])


def swap_other(value):
    pairs = [(i, i + 1) for i in range(1, lax.axis_size("space") - 1, 2)]
    return lax.ppermute(value, "space", pairs + [(j, i) for i, j in pairs])


def local(features, kernel_map, block_count, weight_one, weight_two, cotangent):
    slabs, parts = lax.axis_size("space"), lax.axis_size("chan")
    pairs = parts // 2
    rows, depth = features.shape
    nblocks = rows // BLK
    reach = (nblocks + 2 * HB) * BLK
    offsets, entries = kernel_map.shape[1:3]
    wide = weight_one.shape[2]
    flat = offsets * depth
    share = wide // slabs
    order = [0, 1] + [v for j in range(1, pairs) for v in (2 * j, 2 * j + 1)]
    work = 2 * flat * wide * reach
    blocks = pltpu.VMEM((nblocks + 1, depth, BLK), F32)
    ext = pltpu.VMEM((wide, reach), BF16)

    def reduce_slabs(keep, send):
        got = swap(send, "space", 1)
        outs = call(
            functools.partial(halve_body, "space"),
            [pltpu.VMEM((share, flat), F32)] + [pltpu.VMEM((share, flat), BF16)] * (slabs // 2 - 1),
            [held(keep), held(got)],
            traffic=2 << 20,
        )
        gots = [swap(v, "space", 2 * (j + 1)) for j, v in enumerate(outs[1:])]
        total = call(
            functools.partial(finish_body, len(gots)),
            [jax.ShapeDtypeStruct((offsets, share, depth), F32)],
            [held(v) for v in [outs[0]] + gots],
            traffic=2 << 20,
        )[0]
        return total.transpose(0, 2, 1)

    w_one = weight_one.reshape(flat, wide)
    w_two = weight_two.reshape(flat, wide)

    shard_t = features.T
    far = [swap(shard_t, "chan", 2 * j) for j in range(1, pairs)]
    cot = cotangent.T
    tab, spread_two, keep, send = call(
        input_grad_body,
        [
            pltpu.VMEM((entries + PAD, offsets), jnp.int32),
            pltpu.VMEM((flat, reach), BF16),
            pltpu.VMEM((pairs, depth, reach), BF16),
            pltpu.VMEM((pairs, depth, reach), BF16),
        ],
        [pltpu.with_memory_space_constraint(v, pltpu.HBM) for v in (block_count, kernel_map[0].transpose(2, 1, 0), cot, w_two)],
        [
            pltpu.VMEM((3, entries, offsets), jnp.int32),
            pltpu.VMEM(cot.shape, BF16),
            pltpu.VMEM(w_two.shape, BF16),
            blocks,
            pltpu.VMEM((parts, depth, reach), BF16),
            pltpu.SMEM((entries + PAD, offsets), jnp.int32),
            pltpu.SemaphoreType.DMA((3,)),
            pltpu.SemaphoreType.DMA,
        ],
        vmem=16,
        flops=work,
        traffic=16 << 20,
        specs=[SMEM, FAR, FAR, FAR],
    )
    pieces = [shard_t, swap(shard_t, "chan", 1)]
    for got in far:
        (got,) = call(pass_body, [pltpu.VMEM(got.shape, BF16)], [held(got)], after=[send])
        pieces += [got, swap(got, "chan", 1)]
    x_wide, rim_a, rim_b = call(
        functools.partial(join_body, order),
        [pltpu.VMEM((wide, rows), BF16), pltpu.VMEM((wide, RIM), BF16), pltpu.VMEM((wide, RIM), BF16)],
        [tab] + [held(v) for v in pieces],
        flops=8 * work,
        traffic=2 << 20,
    )
    x_a, x_b = swap(rim_a, "space", 1), swap_other(rim_b)
    got = swap(send, "chan", 1)
    mine, *sends = call(
        functools.partial(halve_body, "chan"),
        [pltpu.VMEM((depth, reach), F32)] + [pltpu.VMEM((depth, reach), BF16)] * (pairs - 1),
        [held(keep), held(got)],
        traffic=2 << 20,
        after=[rim_a],
    )
    gots = [swap(v, "chan", 2 * (j + 1)) for j, v in enumerate(sends)]

    conv_scratch = [ext, pltpu.VMEM((flat, reach), F32)] + [blocks] * 2
    (prod_one,) = call(
        inner_body,
        [pltpu.VMEM((flat, reach), F32)],
        [w_one, held(x_wide)],
        vmem=10,
        flops=work,
        traffic=16 << 20,
        after=[mine],
    )
    z_one, hidden, _ = call(
        hidden_body,
        [pltpu.VMEM((depth, rows), F32), pltpu.VMEM((depth, rows), BF16), pltpu.VMEM((flat, reach), F32)],
        [tab, w_one] + [held(v) for v in (x_a, x_b, prod_one)],
        [blocks] * 2,
        vmem=12,
        flops=work,
        traffic=16 << 20,
        aliases={4: 2},
    )
    far = [swap(hidden, "chan", 2 * j) for j in range(1, pairs)]
    inner, to_a, to_b = call(
        functools.partial(turn_body, len(gots)),
        [pltpu.VMEM((depth, rows), F32), pltpu.VMEM((2, depth, RIM), BF16), pltpu.VMEM((2, depth, RIM), BF16)],
        [tab] + [held(v) for v in [hidden, mine] + gots],
        traffic=2 << 20,
    )
    from_a, from_b = swap(to_a, "space", 1), swap_other(to_b)
    rim, full = call(
        pack_body,
        [pltpu.VMEM((depth, 2 * RIM), BF16), pltpu.VMEM((depth, reach), BF16)],
        [held(v) for v in (hidden, from_a, from_b)],
        traffic=1 << 20,
    )
    far_rims = [swap(rim, "chan", 2 * j) for j in range(1, pairs)]
    full_other = swap(full, "chan", 1)

    grad_outs = [pltpu.VMEM((slabs // 2, share, flat), F32), pltpu.VMEM((slabs // 2, share, flat), BF16)]
    total_scratch = pltpu.VMEM((slabs, share, flat), F32)
    keep_one, send_one = call(
        grad_one_body,
        grad_outs,
        [tab] + [held(v) for v in (z_one, inner, from_a, from_b, x_wide, x_a, x_b)],
        [pltpu.VMEM((depth, rows), F32), blocks, pltpu.VMEM((flat, reach), BF16), ext, total_scratch],
        vmem=26,
        flops=work,
        traffic=16 << 20,
    )
    grad_one = reduce_slabs(keep_one, send_one)

    pieces = [full, full_other]
    for got, got_rim in zip(far, far_rims):
        (got,) = call(
            append_body, [pltpu.VMEM((depth, reach), BF16)], [held(got), held(got_rim)], traffic=1 << 20, after=[keep_one]
        )
        pieces += [got, swap(got, "chan", 1)]
    keep_two, send_two = call(
        functools.partial(grad_two_body, order),
        grad_outs,
        [held(v) for v in [spread_two] + pieces],
        [ext, total_scratch],
        vmem=14,
        flops=work,
        traffic=8 << 20,
    )
    grad_two = reduce_slabs(keep_two, send_two)
    (output,) = call(
        functools.partial(output_body, order),
        [jax.ShapeDtypeStruct((depth, rows), BF16)],
        [tab, w_two] + [held(v) for v in pieces],
        conv_scratch,
        vmem=34,
        flops=work,
        traffic=16 << 20,
    )
    return output.T, grad_one, grad_two


def solution(mesh):
    return jax.shard_map(
        local,
        mesh=mesh,
        in_specs=(
            P("space", "chan"),
            P("space", None, None, None),
            P(),
            P(None, "chan", None),
            P(None, "chan", None),
            P("space", "chan"),
        ),
        out_specs=(P("space", "chan"), P(None, "chan", "space"), P(None, "chan", "space")),
        check_vma=False,
    )
```

```python
import functools

import jax
import jax.numpy as jnp
from jax import lax
from jax.experimental import pallas as pl
from jax.experimental.pallas import tpu as pltpu
from jax.sharding import PartitionSpec as P

BLK = 128
HB = 2
Y_FIRST = 20
RIM = HB * BLK
STEP = 256
F32 = jnp.float32
BF16 = jnp.bfloat16

VMEM = pl.BlockSpec(memory_space=pltpu.VMEM)
SMEM = pl.BlockSpec(memory_space=pltpu.SMEM)
FAR = pl.BlockSpec(memory_space=pltpu.HBM)
PAD = 8


def held(value):
    return pltpu.with_memory_space_constraint(value, pltpu.VMEM)


def call(body, outs, ins, scratch=(), flops=0, traffic=0, vmem=6, specs=None, after=(), aliases=None):
    specs = list(specs or [SMEM if a.dtype == jnp.int32 else VMEM for a in ins])
    first, last = len(ins), len(ins) + len(after)
    ins = list(ins) + [held(v) for v in after]
    specs += [VMEM] * len(after)

    def ordered(*refs):
        body(*refs[:first], *refs[last:])

    name = getattr(body, "func", body).__name__
    kernel = pl.pallas_call(
        ordered,
        out_shape=outs,
        in_specs=specs,
        out_specs=[VMEM] * len(outs),
        scratch_shapes=list(scratch),
        input_output_aliases=aliases or {},
        compiler_params=pltpu.CompilerParams(vmem_limit_bytes=vmem << 20),
        cost_estimate=pl.CostEstimate(flops=flops, bytes_accessed=traffic, transcendentals=0),
    )
    with jax.named_scope(name):
        return kernel(*ins)


def chunks(total, step, body):
    whole = total // step

    def one(i, _):
        body(pl.multiple_of(i * step, step), step)
        return 0

    lax.fori_loop(0, whole, one, 0)
    if total % step:
        body(whole * step, total % step)


def cell(code):
    return code >> 6, code & 63


def near_rim(tab):
    row = tab.shape[0] - PAD
    return pl.multiple_of(tab[row, 0], BLK), pl.multiple_of(tab[row, 1], BLK)


def table(counts, map_ref, nblocks):
    shard = lax.axis_index("space")
    even = shard % 2 == 0
    own_count, left_count = counts[shard], counts[jnp.maximum(shard - 1, 0)]
    source, inblock, target = map_ref[0], map_ref[1], map_ref[2]
    left = jnp.where(even, nblocks + HB, nblocks) - (left_count - HB)
    right = jnp.where(even, nblocks, nblocks + HB)
    position = inblock + jnp.where(source == shard, 0, jnp.where(source < shard, left, right))
    code = position * 64 + jnp.where(target < own_count, target, nblocks)
    entries = code.shape[0]
    index = lax.broadcasted_iota(jnp.int32, code.shape, 0)
    rank = jnp.zeros_like(code)
    for e in range(entries):
        row = code[e : e + 1]
        rank += ((row < code) | ((row == code) & (e < index))).astype(jnp.int32)
    rows = [jnp.sum(jnp.where(rank == e, code, 0), axis=0, keepdims=True) for e in range(entries)]
    tail = (own_count - HB) * BLK
    spot = (lax.broadcasted_iota(jnp.int32, (PAD, code.shape[1]), 1) == 0) == even
    return jnp.concatenate(rows + [jnp.where(spot, tail, 0)], axis=0)


def spread(tab, blocks, spread_ref):
    depth = blocks.shape[1]
    entries, offsets = tab.shape[0] - PAD, tab.shape[1]

    def one(k, _):
        rows = pl.ds(pl.multiple_of(k * depth, depth), depth)
        spread_ref[:, rows, :] = jnp.zeros((spread_ref.shape[0], depth, BLK), BF16)
        before, acc = -1, jnp.zeros((depth, BLK), F32)
        for e in range(entries):
            s, t = cell(tab[e, k])
            acc = jnp.where(s == before, acc, 0.0) + blocks[t]
            spread_ref[s, rows, :] = acc.astype(BF16)
            before = s
        return 0

    lax.fori_loop(0, offsets, one, 0)


def collect(tab, prod, sums):
    depth = sums[0].shape[1]
    entries, offsets = tab.shape[0] - PAD, tab.shape[1]
    for acc in sums:
        acc[...] = jnp.zeros_like(acc)

    def one(k, _):
        rows = pl.ds(pl.multiple_of(k * depth, depth), depth)
        for e in range(entries):
            acc = sums[e % len(sums)]
            s, t = cell(tab[e, k])
            acc[t] = acc[t] + prod[s, rows, :]
        return 0

    lax.fori_loop(0, offsets, one, 0)


def lay(ext_ref, order, refs):
    depth = refs[0].shape[0]
    for bits, ref in zip(order, refs):
        place = lax.axis_index("chan") ^ bits
        ext_ref[pl.ds(pl.multiple_of(place * depth, depth), depth), :] = ref[...]


def extend(ext_ref, wide_ref, a_ref, b_ref):
    rows = wide_ref.shape[1]
    ext_ref[:, :rows] = wide_ref[...]
    ext_ref[:, rows : rows + RIM] = a_ref[...]
    ext_ref[:, rows + RIM :] = b_ref[...]


def input_grad_body(
    counts, map_hbm, cot_hbm, w_hbm, feat_hbm, tab_ref, spread_ref, keep_ref, send_ref,
    own_ref, map_ref, cot_ref, w_ref, blocks, part, tab, sems, sem
):
    ways = [(map_hbm, map_ref), (cot_hbm, cot_ref), (w_hbm, w_ref), (feat_hbm, own_ref)]
    loads = [pltpu.make_async_copy(src, dst, sems.at[i]) for i, (src, dst) in enumerate(ways)]
    for load in loads:
        load.start()
    depth, rows = cot_ref.shape
    nblocks = rows // BLK
    loads[0].wait()
    tab_ref[...] = table(counts, map_ref, nblocks)
    copy = pltpu.make_async_copy(tab_ref, tab, sem)
    copy.start()
    loads[1].wait()
    for b in range(nblocks):
        blocks[b] = cot_ref[:, b * BLK : (b + 1) * BLK].astype(F32)
    blocks[nblocks] = jnp.zeros_like(blocks[nblocks])
    copy.wait()
    spread(tab, blocks, spread_ref)
    loads[2].wait()

    half = spread_ref.shape[0] // 2

    def product(i, _):
        table = jnp.concatenate([spread_ref[i * half + j] for j in range(half)], axis=1)
        res = lax.dot_general(w_ref[...], table, (((0,), (0,)), ((), ())), preferred_element_type=F32)
        cols = pl.ds(pl.multiple_of(i * half * BLK, BLK), half * BLK)
        part[:, :, cols] = res.astype(BF16).reshape(part.shape[0], depth, half * BLK)
        return 0

    lax.fori_loop(0, 2, product, 0)
    core = lax.axis_index("chan") % 2
    for j in range(keep_ref.shape[0]):
        keep_ref[j] = part[2 * j + core]
        send_ref[j] = part[2 * j + 1 - core]
    loads[3].wait()


def pass_body(value_ref, out_ref):
    out_ref[...] = value_ref[...]


def join_body(order, tab, *refs):
    pieces = len(order)
    wide_ref, a_ref, b_ref = refs[pieces:]
    lay(wide_ref, order, refs[:pieces])
    a, b = near_rim(tab)
    a_ref[...] = wide_ref[:, pl.ds(a, RIM)]
    b_ref[...] = wide_ref[:, pl.ds(b, RIM)]


def multiply(w_ref, value, prod, first):
    res = jnp.dot(w_ref[...], value, preferred_element_type=F32)
    for j in range(value.shape[1] // BLK):
        prod[first + j] = res[:, j * BLK : (j + 1) * BLK]


def gather_sums(tab, prod, sums, store):
    collect(tab, prod, sums)
    for b in range(sums[0].shape[0] - 1):
        total = sums[0][b]
        for acc in sums[1:]:
            total = total + acc[b]
        store(slice(b * BLK, (b + 1) * BLK), total)


def inner_body(w_ref, wide_ref, prod_ref):
    multiply(w_ref, wide_ref[...], prod_ref, 0)


def hidden_body(tab, w_ref, a_ref, b_ref, _, z_ref, hidden_ref, prod, *sums):
    nblocks = z_ref.shape[1] // BLK
    multiply(w_ref, jnp.concatenate([a_ref[...], b_ref[...]], axis=1), prod, nblocks)

    def store(cols, z):
        z_ref[:, cols] = z
        hidden_ref[:, cols] = (z / (1.0 + jnp.exp(-z))).astype(BF16)

    gather_sums(tab, prod, sums, store)


def output_body(order, tab, w_ref, *refs):
    pieces = len(order)
    out_ref, done_ref, ext, prod, *sums = refs[pieces:]
    done_ref[...] = jnp.zeros_like(done_ref)
    lay(ext, order, refs[:pieces])

    def store(cols, total):
        out_ref[:, cols] = total.astype(BF16)

    half = prod.shape[0] // 2
    for i in range(2):
        multiply(w_ref, ext[:, i * half * BLK : (i + 1) * half * BLK], prod, i * half)
    gather_sums(tab, prod, sums, store)


def halve_body(axis, keep_ref, got_ref, mine_ref, *send_refs):
    place = lax.axis_index(axis) // 2
    mine_ref[...] = keep_ref[place].astype(F32) + got_ref[place].astype(F32)
    for j, ref in enumerate(send_refs):
        other = place ^ (j + 1)
        ref[...] = (keep_ref[other].astype(F32) + got_ref[other].astype(F32)).astype(BF16)


def turn_body(count, tab, hidden_ref, mine_ref, *refs):
    gots, (inner_ref, a_ref, b_ref) = refs[:count], refs[count:]
    total = mine_ref[...]
    for ref in gots:
        total = total + ref[...].astype(F32)
    rows = inner_ref.shape[1]
    inner_ref[...] = total[:, :rows]
    a, b = near_rim(tab)
    a_ref[0] = total[:, rows : rows + RIM].astype(BF16)
    a_ref[1] = hidden_ref[:, pl.ds(a, RIM)]
    b_ref[0] = total[:, rows + RIM :].astype(BF16)
    b_ref[1] = hidden_ref[:, pl.ds(b, RIM)]


def pack_body(hidden_ref, a_ref, b_ref, rim_ref, full_ref):
    rows = hidden_ref.shape[1]
    rim_ref[:, :RIM] = a_ref[1]
    rim_ref[:, RIM:] = b_ref[1]
    full_ref[:, :rows] = hidden_ref[...]
    full_ref[:, rows:] = rim_ref[...]


def append_body(wide_ref, rim_ref, full_ref):
    rows = wide_ref.shape[1]
    full_ref[:, :rows] = wide_ref[...]
    full_ref[:, rows:] = rim_ref[...]


def weight_grad(ext, spread_ref, total):
    reach = spread_ref.shape[0]

    def product(start, width):
        part = pl.ds(start, width)
        table = jnp.concatenate([spread_ref[s, part, :] for s in range(reach)], axis=1)
        res = lax.dot_general(ext[...], table, (((1,), (1,)), ((), ())), preferred_element_type=F32)
        total[:, :, :, part] = res.reshape(total.shape[:3] + (width,))

    chunks(spread_ref.shape[1], 7 * BLK, product)


def part_slabs(total, keep_ref, send_ref):
    parity = lax.axis_index("space") % 2
    keep_ref[...] = total[:, parity]
    send_ref[...] = total[:, 1 - parity].astype(BF16)


def grad_two_body(order, spread_ref, *refs):
    pieces = len(order)
    keep_ref, send_ref, mine_ref, *send_refs, ext, total = refs[pieces:]
    lay(ext, order, refs[:pieces])
    weight_grad(ext, spread_ref, total)
    cut = keep_ref.shape[2]
    part_slabs(total.at[:, :, :, :cut], keep_ref, send_ref)
    place = lax.axis_index("space") // 2
    mine_ref[...] = total[place, :, :, cut:]
    for j, ref in enumerate(send_refs):
        ref[...] = total[place ^ (j + 1), :, :, cut:].astype(BF16)


def split_body(count, mine_ref, *refs):
    gots, (keep_ref, send_ref) = refs[:count], refs[count:]
    parity = lax.axis_index("space") % 2
    for ref, place in ((keep_ref, parity), (send_ref, 1 - parity)):
        total = mine_ref[place]
        for got in gots:
            total = total + got[place].astype(F32)
        ref[...] = total.astype(ref.dtype)


def grad_one_body(
    tab, z_ref, inner_ref, from_a, from_b, wide_ref, a_ref, b_ref,
    keep_ref, send_ref, grads, blocks, spread_ref, ext, total
):
    extend(ext, wide_ref, a_ref, b_ref)
    grads[...] = inner_ref[...]
    a, b = near_rim(tab)
    for start, ref in ((a, from_a), (b, from_b)):
        grads[:, pl.ds(start, RIM)] = grads[:, pl.ds(start, RIM)] + ref[0].astype(F32)
    nblocks = blocks.shape[0] - 1
    for i in range(nblocks):
        cols = slice(i * BLK, (i + 1) * BLK)
        z = z_ref[:, cols]
        gate = 1.0 / (1.0 + jnp.exp(-z))
        value = grads[:, cols] * gate * (1.0 + z * (1.0 - gate))
        blocks[i] = value.astype(BF16).astype(F32)
    blocks[nblocks] = jnp.zeros_like(blocks[nblocks])
    spread(tab, blocks, spread_ref)
    weight_grad(ext, spread_ref, total)
    part_slabs(total, keep_ref, send_ref)


def finish_body(counts, *refs):
    out_ref = refs[-1]
    depth = out_ref.shape[2]
    k = first = 0
    for count in counts:
        total = refs[first][...]
        for ref in refs[first + 1 : first + count]:
            total = total + ref[...].astype(F32)
        first += count
        for i in range(total.shape[1] // depth):
            out_ref[k] = total[:, i * depth : (i + 1) * depth]
            k += 1


def swap(value, axis, bits):
    return lax.ppermute(value, axis, [(i, i ^ bits) for i in range(lax.axis_size(axis))])


def swap_other(value):
    pairs = [(i, i + 1) for i in range(1, lax.axis_size("space") - 1, 2)]
    return lax.ppermute(value, "space", pairs + [(j, i) for i, j in pairs])


def local(features, kernel_map, block_count, weight_one, weight_two, cotangent):
    slabs, parts = lax.axis_size("space"), lax.axis_size("chan")
    pairs = parts // 2
    rows, depth = features.shape
    nblocks = rows // BLK
    reach = (nblocks + 2 * HB) * BLK
    offsets, entries = kernel_map.shape[1:3]
    wide = weight_one.shape[2]
    flat = offsets * depth
    share = wide // slabs
    order = [0, 1] + [v for j in range(1, pairs) for v in (2 * j, 2 * j + 1)]
    work = 2 * flat * wide * reach
    blocks = pltpu.VMEM((nblocks + 1, depth, BLK), F32)
    ext = pltpu.VMEM((wide, reach), BF16)
    spread_shape = (nblocks + 2 * HB, flat, BLK)

    def finish(*groups):
        total = call(
            functools.partial(finish_body, [len(g) for g in groups]),
            [jax.ShapeDtypeStruct((offsets, share, depth), F32)],
            [held(v) for g in groups for v in g],
            traffic=2 << 20,
        )[0]
        return total.transpose(0, 2, 1)

    def reduce_far(keep, got, after):
        width = keep.shape[2]
        mine, *sends = call(
            functools.partial(halve_body, "space"),
            [pltpu.VMEM((share, width), F32)] + [pltpu.VMEM((share, width), BF16)] * (slabs // 2 - 1),
            [held(keep), held(got)],
            traffic=2 << 20,
            after=after,
        )
        return [mine] + [swap(v, "space", 2 * (j + 1)) for j, v in enumerate(sends)]

    w_one = weight_one.reshape(flat, wide)
    w_two = weight_two.reshape(flat, wide)

    shard_t = features.T
    far = [swap(shard_t, "chan", 2 * j) for j in range(1, pairs)]
    cot = cotangent.T
    tab, spread_two, keep, send, own = call(
        input_grad_body,
        [
            pltpu.VMEM((entries + PAD, offsets), jnp.int32),
            pltpu.VMEM(spread_shape, BF16),
            pltpu.VMEM((pairs, depth, reach), BF16),
            pltpu.VMEM((pairs, depth, reach), BF16),
            pltpu.VMEM((depth, rows), BF16),
        ],
        [
            pltpu.with_memory_space_constraint(v, pltpu.HBM)
            for v in (block_count, kernel_map[0].transpose(2, 1, 0), cot, w_two, shard_t)
        ],
        [
            pltpu.VMEM((3, entries, offsets), jnp.int32),
            pltpu.VMEM(cot.shape, BF16),
            pltpu.VMEM(w_two.shape, BF16),
            blocks,
            pltpu.VMEM((parts, depth, reach), BF16),
            pltpu.SMEM((entries + PAD, offsets), jnp.int32),
            pltpu.SemaphoreType.DMA((4,)),
            pltpu.SemaphoreType.DMA,
        ],
        vmem=16,
        flops=work,
        traffic=16 << 20,
        specs=[SMEM] + [FAR] * 4,
    )
    pieces = [own, swap(shard_t, "chan", 1)]
    for got in far:
        (got,) = call(pass_body, [pltpu.VMEM(got.shape, BF16)], [held(got)], after=[send])
        pieces += [got, swap(got, "chan", 1)]
    x_wide, rim_a, rim_b = call(
        functools.partial(join_body, order),
        [pltpu.VMEM((wide, rows), BF16), pltpu.VMEM((wide, RIM), BF16), pltpu.VMEM((wide, RIM), BF16)],
        [tab] + [held(v) for v in pieces],
        flops=8 * work,
        traffic=2 << 20,
    )
    x_a, x_b = swap(rim_a, "space", 1), swap_other(rim_b)
    got = swap(send, "chan", 1)
    mine, *sends = call(
        functools.partial(halve_body, "chan"),
        [pltpu.VMEM((depth, reach), F32)] + [pltpu.VMEM((depth, reach), BF16)] * (pairs - 1),
        [held(keep), held(got)],
        traffic=2 << 20,
        after=[rim_a],
    )
    gots = [swap(v, "chan", 2 * (j + 1)) for j, v in enumerate(sends)]

    conv_scratch = [ext, pltpu.VMEM(spread_shape, F32)] + [blocks] * 2
    (prod_one,) = call(
        inner_body,
        [pltpu.VMEM(spread_shape, F32)],
        [w_one, held(x_wide)],
        vmem=10,
        flops=work,
        traffic=16 << 20,
        after=[mine],
    )
    z_one, hidden, _ = call(
        hidden_body,
        [pltpu.VMEM((depth, rows), F32), pltpu.VMEM((depth, rows), BF16), pltpu.VMEM(spread_shape, F32)],
        [tab, w_one] + [held(v) for v in (x_a, x_b, prod_one)],
        [blocks] * 2,
        vmem=12,
        flops=work,
        traffic=16 << 20,
        aliases={4: 2},
    )
    far = [swap(hidden, "chan", 2 * j) for j in range(1, pairs)]
    inner, to_a, to_b = call(
        functools.partial(turn_body, len(gots)),
        [pltpu.VMEM((depth, rows), F32), pltpu.VMEM((2, depth, RIM), BF16), pltpu.VMEM((2, depth, RIM), BF16)],
        [tab] + [held(v) for v in [hidden, mine] + gots],
        traffic=2 << 20,
    )
    from_a, from_b = swap(to_a, "space", 1), swap_other(to_b)
    rim, full = call(
        pack_body,
        [pltpu.VMEM((depth, 2 * RIM), BF16), pltpu.VMEM((depth, reach), BF16)],
        [held(v) for v in (hidden, from_a, from_b)],
        traffic=1 << 20,
    )
    far_rims = [swap(rim, "chan", 2 * j) for j in range(1, pairs)]
    full_other = swap(full, "chan", 1)

    total = pltpu.VMEM((slabs // 2, 2, share, flat), F32)
    keep_one, send_one = call(
        grad_one_body,
        [pltpu.VMEM((slabs // 2, share, flat), F32), pltpu.VMEM((slabs // 2, share, flat), BF16)],
        [tab] + [held(v) for v in (z_one, inner, from_a, from_b, x_wide, x_a, x_b)],
        [pltpu.VMEM((depth, rows), F32), blocks, pltpu.VMEM(spread_shape, BF16), ext, total],
        vmem=26,
        flops=work,
        traffic=16 << 20,
    )
    got_one = swap(send_one, "space", 1)

    pieces = [full, full_other]
    for got, got_rim in zip(far, far_rims):
        (got,) = call(
            append_body, [pltpu.VMEM((depth, reach), BF16)], [held(got), held(got_rim)], traffic=1 << 20, after=[keep_one]
        )
        pieces += [got, swap(got, "chan", 1)]
    cut = min(Y_FIRST, offsets) * depth
    far_part = (2, share, flat - cut)
    keep_two, send_two, mine_far, *sends_far = call(
        functools.partial(grad_two_body, order),
        [
            pltpu.VMEM((slabs // 2, share, cut), F32),
            pltpu.VMEM((slabs // 2, share, cut), BF16),
            pltpu.VMEM(far_part, F32),
        ]
        + [pltpu.VMEM(far_part, BF16)] * (slabs // 2 - 1),
        [held(v) for v in [spread_two] + pieces],
        [ext, total],
        vmem=14,
        flops=work,
        traffic=8 << 20,
    )
    gots_far = [swap(v, "space", 2 * (j + 1)) for j, v in enumerate(sends_far)]
    got_two = swap(send_two, "space", 1)
    group_one = reduce_far(keep_one, got_one, [])
    output, done = call(
        functools.partial(output_body, order),
        [jax.ShapeDtypeStruct((depth, rows), BF16), pltpu.VMEM((8, BLK), F32)],
        [tab, w_two] + [held(v) for v in pieces],
        conv_scratch,
        vmem=34,
        flops=8 * work,
        traffic=16 << 20,
        after=[group_one[0]],
    )
    keep_far, send_far = call(
        functools.partial(split_body, len(gots_far)),
        [pltpu.VMEM(far_part[1:], F32), pltpu.VMEM(far_part[1:], BF16)],
        [held(v) for v in [mine_far] + gots_far],
        traffic=1 << 20,
        after=[done],
    )
    got_far = swap(send_far, "space", 1)
    group_two = reduce_far(keep_two, got_two, [keep_far])
    grad_one = finish(group_one)
    grad_two = finish(group_two, [keep_far, got_far])
    return output.T, grad_one, grad_two


def solution(mesh):
    return jax.shard_map(
        local,
        mesh=mesh,
        in_specs=(
            P("space", "chan"),
            P("space", None, None, None),
            P(),
            P(None, "chan", None),
            P(None, "chan", None),
            P("space", "chan"),
        ),
        out_specs=(P("space", "chan"), P(None, "chan", "space"), P(None, "chan", "space")),
        check_vma=False,
    )
```

```python
import functools

import jax
import jax.numpy as jnp
from jax import lax
from jax.experimental import pallas as pl
from jax.experimental.pallas import tpu as pltpu
from jax.sharding import PartitionSpec as P

BLK = 128
HB = 2
Y_FIRST = 20
RIM = HB * BLK
STEP = 256
F32 = jnp.float32
BF16 = jnp.bfloat16

VMEM = pl.BlockSpec(memory_space=pltpu.VMEM)
SMEM = pl.BlockSpec(memory_space=pltpu.SMEM)
FAR = pl.BlockSpec(memory_space=pltpu.HBM)
PAD = 8


def held(value):
    return pltpu.with_memory_space_constraint(value, pltpu.VMEM)


def call(body, outs, ins, scratch=(), flops=0, traffic=0, vmem=6, specs=None, after=(), aliases=None):
    specs = list(specs or [SMEM if a.dtype == jnp.int32 else VMEM for a in ins])
    first, last = len(ins), len(ins) + len(after)
    ins = list(ins) + [held(v) for v in after]
    specs += [VMEM] * len(after)

    def ordered(*refs):
        body(*refs[:first], *refs[last:])

    name = getattr(body, "func", body).__name__
    kernel = pl.pallas_call(
        ordered,
        out_shape=outs,
        in_specs=specs,
        out_specs=[VMEM] * len(outs),
        scratch_shapes=list(scratch),
        input_output_aliases=aliases or {},
        compiler_params=pltpu.CompilerParams(vmem_limit_bytes=vmem << 20),
        cost_estimate=pl.CostEstimate(flops=flops, bytes_accessed=traffic, transcendentals=0),
    )
    with jax.named_scope(name):
        return kernel(*ins)


def chunks(total, step, body):
    whole = total // step

    def one(i, _):
        body(pl.multiple_of(i * step, step), step)
        return 0

    lax.fori_loop(0, whole, one, 0)
    if total % step:
        body(whole * step, total % step)


def cell(code):
    return code >> 6, code & 63


def near_rim(tab):
    row = tab.shape[0] - PAD
    return pl.multiple_of(tab[row, 0], BLK), pl.multiple_of(tab[row, 1], BLK)


def table(counts, map_ref, nblocks):
    shard = lax.axis_index("space")
    even = shard % 2 == 0
    own_count, left_count = counts[shard], counts[jnp.maximum(shard - 1, 0)]
    source, inblock, target = map_ref[0], map_ref[1], map_ref[2]
    left = jnp.where(even, nblocks + HB, nblocks) - (left_count - HB)
    right = jnp.where(even, nblocks, nblocks + HB)
    position = inblock + jnp.where(source == shard, 0, jnp.where(source < shard, left, right))
    code = position * 64 + jnp.where(target < own_count, target, nblocks)
    entries = code.shape[0]
    index = lax.broadcasted_iota(jnp.int32, code.shape, 0)
    rank = jnp.zeros_like(code)
    for e in range(entries):
        row = code[e : e + 1]
        rank += ((row < code) | ((row == code) & (e < index))).astype(jnp.int32)
    rows = [jnp.sum(jnp.where(rank == e, code, 0), axis=0, keepdims=True) for e in range(entries)]
    tail = (own_count - HB) * BLK
    spot = (lax.broadcasted_iota(jnp.int32, (PAD, code.shape[1]), 1) == 0) == even
    return jnp.concatenate(rows + [jnp.where(spot, tail, 0)], axis=0)


def spread(tab, blocks, spread_ref):
    depth = blocks.shape[1]
    entries, offsets = tab.shape[0] - PAD, tab.shape[1]

    def one(k):
        rows = slice(k * depth, (k + 1) * depth)
        spread_ref[:, rows, :] = jnp.zeros((spread_ref.shape[0], depth, BLK), BF16)
        before, acc = -1, jnp.zeros((depth, BLK), F32)
        for e in range(entries):
            s, t = cell(tab[e, k])
            acc = jnp.where(s == before, acc, 0.0) + blocks[t]
            spread_ref[s, rows, :] = acc.astype(BF16)
            before = s

    for k in range(offsets):
        one(k)


def collect(tab, prod, sums):
    depth = sums[0].shape[1]
    entries, offsets = tab.shape[0] - PAD, tab.shape[1]
    for acc in sums:
        acc[...] = jnp.zeros_like(acc)

    def one(k, _):
        rows = pl.ds(pl.multiple_of(k * depth, depth), depth)
        for e in range(entries):
            acc = sums[e % len(sums)]
            s, t = cell(tab[e, k])
            acc[t] = acc[t] + prod[s, rows, :]
        return 0

    lax.fori_loop(0, offsets, one, 0)


def lay(ext_ref, order, refs):
    depth = refs[0].shape[0]
    for bits, ref in zip(order, refs):
        place = lax.axis_index("chan") ^ bits
        ext_ref[pl.ds(pl.multiple_of(place * depth, depth), depth), :] = ref[...]


def input_grad_body(
    counts, map_hbm, cot_hbm, w_hbm, feat_hbm, tab_ref, spread_ref, keep_ref, send_ref,
    own_ref, map_ref, cot_ref, w_ref, blocks, part, tab, sems, sem
):
    ways = [(map_hbm, map_ref), (cot_hbm, cot_ref), (w_hbm, w_ref), (feat_hbm, own_ref)]
    loads = [pltpu.make_async_copy(src, dst, sems.at[i]) for i, (src, dst) in enumerate(ways)]
    for load in loads:
        load.start()
    depth, rows = cot_ref.shape
    nblocks = rows // BLK
    loads[0].wait()
    tab_ref[...] = table(counts, map_ref, nblocks)
    copy = pltpu.make_async_copy(tab_ref, tab, sem)
    copy.start()
    loads[1].wait()
    for b in range(nblocks):
        blocks[b] = cot_ref[:, b * BLK : (b + 1) * BLK].astype(F32)
    blocks[nblocks] = jnp.zeros_like(blocks[nblocks])
    copy.wait()
    spread(tab, blocks, spread_ref)
    loads[2].wait()

    half = spread_ref.shape[0] // 2

    def product(i, _):
        table = jnp.concatenate([spread_ref[i * half + j] for j in range(half)], axis=1)
        res = lax.dot_general(w_ref[...], table, (((0,), (0,)), ((), ())), preferred_element_type=F32)
        cols = pl.ds(pl.multiple_of(i * half * BLK, BLK), half * BLK)
        part[:, :, cols] = res.astype(BF16).reshape(part.shape[0], depth, half * BLK)
        return 0

    lax.fori_loop(0, 2, product, 0)
    core = lax.axis_index("chan") % 2
    for j in range(keep_ref.shape[0]):
        keep_ref[j] = part[2 * j + core]
        send_ref[j] = part[2 * j + 1 - core]
    loads[3].wait()


def pass_body(value_ref, out_ref):
    out_ref[...] = value_ref[...]


def cut_body(order, tab, *refs):
    pieces = len(order)
    a_ref, b_ref, rims = refs[pieces:]
    depth, half = refs[0].shape[0], a_ref.shape[0]
    own = pl.ds(pl.multiple_of(lax.axis_index("chan") % 2 * half, half), half)
    for start, out_ref in zip(near_rim(tab), (a_ref, b_ref)):
        for bits, ref in zip(order, refs[:pieces]):
            place = lax.axis_index("chan") ^ bits
            rims[pl.ds(pl.multiple_of(place * depth, depth), depth), :] = ref[:, pl.ds(start, RIM)]
        out_ref[...] = rims[own, :]


def multiply(w_ref, value, prod, first):
    res = jnp.dot(w_ref[...], value, preferred_element_type=F32)
    for j in range(value.shape[1] // BLK):
        prod[first + j] = res[:, j * BLK : (j + 1) * BLK]


def gather_sums(tab, prod, sums, store):
    collect(tab, prod, sums)
    for b in range(sums[0].shape[0] - 1):
        total = sums[0][b]
        for acc in sums[1:]:
            total = total + acc[b]
        store(slice(b * BLK, (b + 1) * BLK), total)


def inner_body(order, w_ref, *refs):
    pieces = len(order)
    prod_ref, wide_ref = refs[pieces:]
    lay(wide_ref, order, refs[:pieces])
    multiply(w_ref, wide_ref[...], prod_ref, 0)


def stack_body(a_ref, b_ref, out_ref):
    out_ref[:, :RIM] = a_ref[...]
    out_ref[:, RIM:] = b_ref[...]


def hidden_body(tab, w_ref, own_ref, other_ref, _, z_ref, hidden_ref, rims_ref, prod, *sums):
    core, half = lax.axis_index("chan") % 2, own_ref.shape[0]
    for place, ref in ((core, own_ref), (1 - core, other_ref)):
        rims_ref[pl.ds(pl.multiple_of(place * half, half), half), :] = ref[...]
    multiply(w_ref, rims_ref[...], prod, z_ref.shape[1] // BLK)

    def store(cols, z):
        z_ref[:, cols] = z
        hidden_ref[:, cols] = (z / (1.0 + jnp.exp(-z))).astype(BF16)

    gather_sums(tab, prod, sums, store)


def output_body(order, tab, w_ref, *refs):
    pieces = len(order)
    out_ref, done_ref, ext, prod, *sums = refs[pieces:]
    done_ref[...] = jnp.zeros_like(done_ref)
    lay(ext, order, refs[:pieces])

    def store(cols, total):
        out_ref[:, cols] = total.astype(BF16)

    half = prod.shape[0] // 2
    for i in range(2):
        multiply(w_ref, ext[:, i * half * BLK : (i + 1) * half * BLK], prod, i * half)
    gather_sums(tab, prod, sums, store)


def halve_body(axis, keep_ref, got_ref, mine_ref, *send_refs):
    place = lax.axis_index(axis) // 2
    mine_ref[...] = keep_ref[place].astype(F32) + got_ref[place].astype(F32)
    for j, ref in enumerate(send_refs):
        other = place ^ (j + 1)
        ref[...] = (keep_ref[other].astype(F32) + got_ref[other].astype(F32)).astype(BF16)


def turn_body(count, tab, hidden_ref, mine_ref, *refs):
    gots, outs = refs[:count], refs[count:]
    rows = hidden_ref.shape[1]
    for i, (start, out_ref) in enumerate(zip(near_rim(tab), outs)):
        cols = slice(rows + i * RIM, rows + (i + 1) * RIM)
        total = mine_ref[:, cols]
        for ref in gots:
            total = total + ref[:, cols].astype(F32)
        out_ref[0] = total.astype(BF16)
        out_ref[1] = hidden_ref[:, pl.ds(start, RIM)]


def pack_body(hidden_ref, a_ref, b_ref, rim_ref, full_ref):
    rows = hidden_ref.shape[1]
    rim_ref[:, :RIM] = a_ref[1]
    rim_ref[:, RIM:] = b_ref[1]
    full_ref[:, :rows] = hidden_ref[...]
    full_ref[:, rows:] = rim_ref[...]


def append_body(wide_ref, rim_ref, full_ref):
    rows = wide_ref.shape[1]
    full_ref[:, :rows] = wide_ref[...]
    full_ref[:, rows:] = rim_ref[...]


def weight_grad(ext_ref, spread_ref, start, width):
    part = pl.ds(start, width)
    table = jnp.concatenate([spread_ref[s, part, :] for s in range(spread_ref.shape[0])], axis=1)
    res = lax.dot_general(ext_ref[...], table, (((1,), (1,)), ((), ())), preferred_element_type=F32)
    slabs = lax.axis_size("space")
    return res.reshape(slabs // 2, 2, res.shape[0] // slabs, width)


def part_slabs(ext_ref, spread_ref, keep_ref, send_ref, step):
    even = lax.axis_index("space") % 2 == 0

    def product(start, width):
        res = weight_grad(ext_ref, spread_ref, start, width)
        part = pl.ds(start, width)
        keep_ref[:, :, part] = jnp.where(even, res[:, 0], res[:, 1])
        send_ref[:, :, part] = jnp.where(even, res[:, 1], res[:, 0]).astype(BF16)

    chunks(keep_ref.shape[2], step, product)


def grad_two_body(order, spread_ref, *refs):
    pieces = len(order)
    keep_ref, send_ref, mine_ref, *send_refs, ext, total = refs[pieces:]
    lay(ext, order, refs[:pieces])
    cut = keep_ref.shape[2]
    part_slabs(ext, spread_ref, keep_ref, send_ref, cut)
    total[...] = weight_grad(ext, spread_ref, cut, mine_ref.shape[2])
    place = lax.axis_index("space") // 2
    mine_ref[...] = total[place]
    for j, ref in enumerate(send_refs):
        ref[...] = total[place ^ (j + 1)].astype(BF16)


def split_body(count, mine_ref, *refs):
    gots, (keep_ref, send_ref) = refs[:count], refs[count:]
    parity = lax.axis_index("space") % 2
    for ref, place in ((keep_ref, parity), (send_ref, 1 - parity)):
        total = mine_ref[place]
        for got in gots:
            total = total + got[place].astype(F32)
        ref[...] = total.astype(ref.dtype)


def prepare_body(z_ref, wide_ref, rims_ref, slope_ref, ext_ref):
    rows = wide_ref.shape[1]
    ext_ref[:, :rows] = wide_ref[...]
    ext_ref[:, rows:] = rims_ref[...]
    z = z_ref[...]
    gate = 1.0 / (1.0 + jnp.exp(-z))
    slope_ref[...] = gate * (1.0 + z * (1.0 - gate))


def grad_one_body(count, tab, slope_ref, from_a, from_b, ext_ref, mine_ref, *refs):
    gots, (keep_ref, send_ref, grads, blocks, spread_ref) = refs[:count], refs[count:]
    rows = slope_ref.shape[1]
    inner = mine_ref[:, :rows]
    for ref in gots:
        inner = inner + ref[:, :rows].astype(F32)
    grads[...] = inner
    a, b = near_rim(tab)
    for start, ref in ((a, from_a), (b, from_b)):
        grads[:, pl.ds(start, RIM)] = grads[:, pl.ds(start, RIM)] + ref[0].astype(F32)
    nblocks = blocks.shape[0] - 1
    for i in range(nblocks):
        cols = slice(i * BLK, (i + 1) * BLK)
        blocks[i] = (grads[:, cols] * slope_ref[:, cols]).astype(BF16).astype(F32)
    blocks[nblocks] = jnp.zeros_like(blocks[nblocks])
    spread(tab, blocks, spread_ref)
    part_slabs(ext_ref, spread_ref, keep_ref, send_ref, 7 * BLK)


def finish_body(counts, *refs):
    out_ref = refs[-1]
    depth = out_ref.shape[2]
    k = first = 0
    for count in counts:
        total = refs[first][...]
        for ref in refs[first + 1 : first + count]:
            total = total + ref[...].astype(F32)
        first += count
        for i in range(total.shape[1] // depth):
            out_ref[k] = total[:, i * depth : (i + 1) * depth]
            k += 1


def swap(value, axis, bits):
    return lax.ppermute(value, axis, [(i, i ^ bits) for i in range(lax.axis_size(axis))])


def swap_other(value):
    pairs = [(i, i + 1) for i in range(1, lax.axis_size("space") - 1, 2)]
    return lax.ppermute(value, "space", pairs + [(j, i) for i, j in pairs])


def local(features, kernel_map, block_count, weight_one, weight_two, cotangent):
    slabs, parts = lax.axis_size("space"), lax.axis_size("chan")
    pairs = parts // 2
    rows, depth = features.shape
    nblocks = rows // BLK
    reach = (nblocks + 2 * HB) * BLK
    offsets, entries = kernel_map.shape[1:3]
    wide = weight_one.shape[2]
    flat = offsets * depth
    share = wide // slabs
    order = [0, 1] + [v for j in range(1, pairs) for v in (2 * j, 2 * j + 1)]
    work = 2 * flat * wide * reach
    blocks = pltpu.VMEM((nblocks + 1, depth, BLK), F32)
    ext = pltpu.VMEM((wide, reach), BF16)
    spread_shape = (nblocks + 2 * HB, flat, BLK)

    def finish(*groups):
        total = call(
            functools.partial(finish_body, [len(g) for g in groups]),
            [jax.ShapeDtypeStruct((offsets, share, depth), F32)],
            [held(v) for g in groups for v in g],
            traffic=2 << 20,
        )[0]
        return total.transpose(0, 2, 1)

    def reduce_far(keep, got, after):
        width = keep.shape[2]
        mine, *sends = call(
            functools.partial(halve_body, "space"),
            [pltpu.VMEM((share, width), F32)] + [pltpu.VMEM((share, width), BF16)] * (slabs // 2 - 1),
            [held(keep), held(got)],
            traffic=2 << 20,
            after=after,
        )
        return [mine] + [swap(v, "space", 2 * (j + 1)) for j, v in enumerate(sends)]

    w_one = weight_one.reshape(flat, wide)
    w_two = weight_two.reshape(flat, wide)

    shard_t = features.T
    far = [swap(shard_t, "chan", 2 * j) for j in range(1, pairs)]
    cot = cotangent.T
    tab, spread_two, keep, send, own = call(
        input_grad_body,
        [
            pltpu.VMEM((entries + PAD, offsets), jnp.int32),
            pltpu.VMEM(spread_shape, BF16),
            pltpu.VMEM((pairs, depth, reach), BF16),
            pltpu.VMEM((pairs, depth, reach), BF16),
            pltpu.VMEM((depth, rows), BF16),
        ],
        [
            pltpu.with_memory_space_constraint(v, pltpu.HBM)
            for v in (block_count, kernel_map[0].transpose(2, 1, 0), cot, w_two, shard_t)
        ],
        [
            pltpu.VMEM((3, entries, offsets), jnp.int32),
            pltpu.VMEM(cot.shape, BF16),
            pltpu.VMEM(w_two.shape, BF16),
            blocks,
            pltpu.VMEM((parts, depth, reach), BF16),
            pltpu.SMEM((entries + PAD, offsets), jnp.int32),
            pltpu.SemaphoreType.DMA((4,)),
            pltpu.SemaphoreType.DMA,
        ],
        vmem=16,
        flops=work,
        traffic=16 << 20,
        specs=[SMEM] + [FAR] * 4,
    )
    pieces = [own, swap(shard_t, "chan", 1)]
    for got in far:
        (got,) = call(pass_body, [pltpu.VMEM(got.shape, BF16)], [held(got)], after=[send])
        pieces += [got, swap(got, "chan", 1)]
    half_rim = pltpu.VMEM((wide // 2, RIM), BF16)
    rim_a, rim_b = call(
        functools.partial(cut_body, order),
        [half_rim, half_rim],
        [tab] + [held(v) for v in pieces],
        [pltpu.VMEM((wide, RIM), BF16)],
        flops=8 * work,
    )
    x_a, x_b = swap(rim_a, "space", 1), swap_other(rim_b)
    got = swap(send, "chan", 1)
    mine, *sends = call(
        functools.partial(halve_body, "chan"),
        [pltpu.VMEM((depth, reach), F32)] + [pltpu.VMEM((depth, reach), BF16)] * (pairs - 1),
        [held(keep), held(got)],
        traffic=2 << 20,
        after=[rim_a],
    )
    gots = [swap(v, "chan", 2 * (j + 1)) for j, v in enumerate(sends)]

    conv_scratch = [ext, pltpu.VMEM(spread_shape, F32)] + [blocks] * 2
    prod_one, x_wide = call(
        functools.partial(inner_body, order),
        [pltpu.VMEM(spread_shape, F32), pltpu.VMEM((wide, rows), BF16)],
        [w_one] + [held(v) for v in pieces],
        vmem=10,
        flops=work,
        traffic=16 << 20,
        after=[mine],
    )
    (x_half,) = call(
        stack_body, [pltpu.VMEM((wide // 2, 2 * RIM), BF16)], [held(x_a), held(x_b)], after=[x_wide]
    )
    z_one, hidden, x_rims, _ = call(
        hidden_body,
        [pltpu.VMEM((depth, rows), F32), pltpu.VMEM((depth, rows), BF16), pltpu.VMEM((wide, 2 * RIM), BF16), pltpu.VMEM(spread_shape, F32)],
        [tab, w_one] + [held(v) for v in (x_half, swap(x_half, "chan", 1), prod_one)],
        [blocks] * 2,
        vmem=12,
        aliases={4: 3},
    )
    far = [swap(hidden, "chan", 2 * j) for j in range(1, pairs)]
    to_a, to_b = call(
        functools.partial(turn_body, len(gots)),
        [pltpu.VMEM((2, depth, RIM), BF16), pltpu.VMEM((2, depth, RIM), BF16)],
        [tab] + [held(v) for v in [hidden, mine] + gots],
        traffic=2 << 20,
    )
    from_a, from_b = swap(to_a, "space", 1), swap_other(to_b)
    rim, full = call(
        pack_body,
        [pltpu.VMEM((depth, 2 * RIM), BF16), pltpu.VMEM((depth, reach), BF16)],
        [held(v) for v in (hidden, from_a, from_b)],
        traffic=1 << 20,
    )
    far_rims = [swap(rim, "chan", 2 * j) for j in range(1, pairs)]
    full_other = swap(full, "chan", 1)

    slope, x_ext = call(
        prepare_body,
        [pltpu.VMEM((depth, rows), F32), pltpu.VMEM((wide, reach), BF16)],
        [held(v) for v in (z_one, x_wide, x_rims)],
        after=[to_a],
    )
    keep_one, send_one = call(
        functools.partial(grad_one_body, len(gots)),
        [pltpu.VMEM((slabs // 2, share, flat), F32), pltpu.VMEM((slabs // 2, share, flat), BF16)],
        [tab] + [held(v) for v in [slope, from_a, from_b, x_ext, mine] + gots],
        [pltpu.VMEM((depth, rows), F32), blocks, pltpu.VMEM(spread_shape, BF16)],
        vmem=24,
        flops=work,
        traffic=16 << 20,
    )
    got_one = swap(send_one, "space", 1)

    pieces = [full, full_other]
    for got, got_rim in zip(far, far_rims):
        (got,) = call(
            append_body, [pltpu.VMEM((depth, reach), BF16)], [held(got), held(got_rim)], traffic=1 << 20, after=[keep_one]
        )
        pieces += [got, swap(got, "chan", 1)]
    cut = min(Y_FIRST, offsets) * depth
    far_part = (2, share, flat - cut)
    keep_two, send_two, mine_far, *sends_far = call(
        functools.partial(grad_two_body, order),
        [
            pltpu.VMEM((slabs // 2, share, cut), F32),
            pltpu.VMEM((slabs // 2, share, cut), BF16),
            pltpu.VMEM(far_part, F32),
        ]
        + [pltpu.VMEM(far_part, BF16)] * (slabs // 2 - 1),
        [held(v) for v in [spread_two] + pieces],
        [ext, pltpu.VMEM((slabs // 2,) + far_part, F32)],
        vmem=14,
    )
    gots_far = [swap(v, "space", 2 * (j + 1)) for j, v in enumerate(sends_far)]
    got_two = swap(send_two, "space", 1)
    group_one = reduce_far(keep_one, got_one, [])
    output, done = call(
        functools.partial(output_body, order),
        [jax.ShapeDtypeStruct((depth, rows), BF16), pltpu.VMEM((8, BLK), F32)],
        [tab, w_two] + [held(v) for v in pieces],
        conv_scratch,
        vmem=34,
        flops=8 * work,
        traffic=16 << 20,
        after=[group_one[0]],
    )
    keep_far, send_far = call(
        functools.partial(split_body, len(gots_far)),
        [pltpu.VMEM(far_part[1:], F32), pltpu.VMEM(far_part[1:], BF16)],
        [held(v) for v in [mine_far] + gots_far],
        traffic=1 << 20,
        after=[done],
    )
    got_far = swap(send_far, "space", 1)
    group_two = reduce_far(keep_two, got_two, [keep_far])
    grad_one = finish(group_one)
    grad_two = finish(group_two, [keep_far, got_far])
    return output.T, grad_one, grad_two


def solution(mesh):
    return jax.shard_map(
        local,
        mesh=mesh,
        in_specs=(
            P("space", "chan"),
            P("space", None, None, None),
            P(),
            P(None, "chan", None),
            P(None, "chan", None),
            P("space", "chan"),
        ),
        out_specs=(P("space", "chan"), P(None, "chan", "space"), P(None, "chan", "space")),
        check_vma=False,
    )
```

```python
import functools

import jax
import jax.numpy as jnp
from jax import lax
from jax.experimental import pallas as pl
from jax.experimental.pallas import tpu as pltpu
from jax.sharding import PartitionSpec as P

BLK = 128
HB = 2
Y_FIRST = 24
RIM = HB * BLK
STEP = 256
F32 = jnp.float32
BF16 = jnp.bfloat16

VMEM = pl.BlockSpec(memory_space=pltpu.VMEM)
SMEM = pl.BlockSpec(memory_space=pltpu.SMEM)
FAR = pl.BlockSpec(memory_space=pltpu.HBM)
PAD = 8


def held(value):
    return pltpu.with_memory_space_constraint(value, pltpu.VMEM)


def call(body, outs, ins, scratch=(), flops=0, traffic=0, vmem=6, specs=None, after=(), aliases=None):
    specs = list(specs or [SMEM if a.dtype == jnp.int32 else VMEM for a in ins])
    first, last = len(ins), len(ins) + len(after)
    ins = list(ins) + [held(v) for v in after]
    specs += [VMEM] * len(after)

    def ordered(*refs):
        body(*refs[:first], *refs[last:])

    name = getattr(body, "func", body).__name__
    kernel = pl.pallas_call(
        ordered,
        out_shape=outs,
        in_specs=specs,
        out_specs=[VMEM] * len(outs),
        scratch_shapes=list(scratch),
        input_output_aliases=aliases or {},
        compiler_params=pltpu.CompilerParams(vmem_limit_bytes=vmem << 20),
        cost_estimate=pl.CostEstimate(flops=flops, bytes_accessed=traffic, transcendentals=0),
    )
    with jax.named_scope(name):
        return kernel(*ins)


def chunks(total, step, body):
    whole = total // step

    def one(i, _):
        body(pl.multiple_of(i * step, step), step)
        return 0

    lax.fori_loop(0, whole, one, 0)
    if total % step:
        body(whole * step, total % step)


def cell(code):
    return code >> 6, code & 63


def near_rim(tab):
    row = tab.shape[0] - PAD
    return pl.multiple_of(tab[row, 0], BLK), pl.multiple_of(tab[row, 1], BLK)


def table(counts, map_ref, nblocks):
    shard = lax.axis_index("space")
    even = shard % 2 == 0
    own_count, left_count = counts[shard], counts[jnp.maximum(shard - 1, 0)]
    source, inblock, target = map_ref[0], map_ref[1], map_ref[2]
    left = jnp.where(even, nblocks + HB, nblocks) - (left_count - HB)
    right = jnp.where(even, nblocks, nblocks + HB)
    position = inblock + jnp.where(source == shard, 0, jnp.where(source < shard, left, right))
    code = position * 64 + jnp.where(target < own_count, target, nblocks)
    entries = code.shape[0]
    index = lax.broadcasted_iota(jnp.int32, code.shape, 0)
    rank = jnp.zeros_like(code)
    for e in range(entries):
        row = code[e : e + 1]
        rank += ((row < code) | ((row == code) & (e < index))).astype(jnp.int32)
    rows = [jnp.sum(jnp.where(rank == e, code, 0), axis=0, keepdims=True) for e in range(entries)]
    tail = (own_count - HB) * BLK
    spot = (lax.broadcasted_iota(jnp.int32, (PAD, code.shape[1]), 1) == 0) == even
    return jnp.concatenate(rows + [jnp.where(spot, tail, 0)], axis=0)


def spread(tab, blocks, spread_ref):
    depth = blocks.shape[1]
    entries, offsets = tab.shape[0] - PAD, tab.shape[1]

    def one(k):
        rows = slice(k * depth, (k + 1) * depth)
        spread_ref[:, rows, :] = jnp.zeros((spread_ref.shape[0], depth, BLK), BF16)
        before, acc = -1, jnp.zeros((depth, BLK), F32)
        for e in range(entries):
            s, t = cell(tab[e, k])
            acc = jnp.where(s == before, acc, 0.0) + blocks[t]
            spread_ref[s, rows, :] = acc.astype(BF16)
            before = s

    for k in range(offsets):
        one(k)


def collect(tab, prod, sums):
    depth = sums[0].shape[1]
    entries, offsets = tab.shape[0] - PAD, tab.shape[1]
    for acc in sums:
        acc[...] = jnp.zeros_like(acc)

    def one(k, _):
        rows = pl.ds(pl.multiple_of(k * depth, depth), depth)
        for e in range(entries):
            acc = sums[e % len(sums)]
            s, t = cell(tab[e, k])
            acc[t] = acc[t] + prod[s, rows, :]
        return 0

    lax.fori_loop(0, offsets, one, 0)


def lay(ext_ref, order, refs):
    depth = refs[0].shape[0]
    for bits, ref in zip(order, refs):
        place = lax.axis_index("chan") ^ bits
        ext_ref[pl.ds(pl.multiple_of(place * depth, depth), depth), :] = ref[...]


def input_grad_body(
    counts, map_hbm, cot_hbm, w_hbm, feat_hbm, tab_ref, spread_ref, keep_ref, send_ref,
    own_ref, map_ref, cot_ref, w_ref, blocks, part, tab, sems, sem
):
    ways = [(map_hbm, map_ref), (cot_hbm, cot_ref), (w_hbm, w_ref), (feat_hbm, own_ref)]
    loads = [pltpu.make_async_copy(src, dst, sems.at[i]) for i, (src, dst) in enumerate(ways)]
    for load in loads:
        load.start()
    depth, rows = cot_ref.shape
    nblocks = rows // BLK
    loads[0].wait()
    tab_ref[...] = table(counts, map_ref, nblocks)
    copy = pltpu.make_async_copy(tab_ref, tab, sem)
    copy.start()
    loads[1].wait()
    for b in range(nblocks):
        blocks[b] = cot_ref[:, b * BLK : (b + 1) * BLK].astype(F32)
    blocks[nblocks] = jnp.zeros_like(blocks[nblocks])
    copy.wait()
    spread(tab, blocks, spread_ref)
    loads[2].wait()

    half = spread_ref.shape[0] // 2

    def product(i, _):
        table = jnp.concatenate([spread_ref[i * half + j] for j in range(half)], axis=1)
        res = lax.dot_general(w_ref[...], table, (((0,), (0,)), ((), ())), preferred_element_type=F32)
        cols = pl.ds(pl.multiple_of(i * half * BLK, BLK), half * BLK)
        part[:, :, cols] = res.astype(BF16).reshape(part.shape[0], depth, half * BLK)
        return 0

    lax.fori_loop(0, 2, product, 0)
    core = lax.axis_index("chan") % 2
    for j in range(keep_ref.shape[0]):
        keep_ref[j] = part[2 * j + core]
        send_ref[j] = part[2 * j + 1 - core]
    loads[3].wait()


def pass_body(value_ref, out_ref):
    out_ref[...] = value_ref[...]


def cut_body(order, tab, *refs):
    pieces = len(order)
    a_ref, b_ref, rims = refs[pieces:]
    depth, half = refs[0].shape[0], a_ref.shape[0]
    own = pl.ds(pl.multiple_of(lax.axis_index("chan") % 2 * half, half), half)
    for start, out_ref in zip(near_rim(tab), (a_ref, b_ref)):
        for bits, ref in zip(order, refs[:pieces]):
            place = lax.axis_index("chan") ^ bits
            rims[pl.ds(pl.multiple_of(place * depth, depth), depth), :] = ref[:, pl.ds(start, RIM)]
        out_ref[...] = rims[own, :]


def multiply(w_ref, value, prod, first):
    res = jnp.dot(w_ref[...], value, preferred_element_type=F32)
    for j in range(value.shape[1] // BLK):
        prod[first + j] = res[:, j * BLK : (j + 1) * BLK]


def gather_sums(tab, prod, sums, store):
    collect(tab, prod, sums)
    for b in range(sums[0].shape[0] - 1):
        total = sums[0][b]
        for acc in sums[1:]:
            total = total + acc[b]
        store(slice(b * BLK, (b + 1) * BLK), total)


def inner_body(order, w_ref, *refs):
    pieces = len(order)
    prod_ref, wide_ref = refs[pieces:]
    lay(wide_ref, order, refs[:pieces])
    multiply(w_ref, wide_ref[...], prod_ref, 0)


def stack_body(a_ref, b_ref, out_ref):
    out_ref[:, :RIM] = a_ref[...]
    out_ref[:, RIM:] = b_ref[...]


def hidden_body(tab, w_ref, own_ref, other_ref, _, z_ref, hidden_ref, rims_ref, prod, *sums):
    core, half = lax.axis_index("chan") % 2, own_ref.shape[0]
    for place, ref in ((core, own_ref), (1 - core, other_ref)):
        rims_ref[pl.ds(pl.multiple_of(place * half, half), half), :] = ref[...]
    multiply(w_ref, rims_ref[...], prod, z_ref.shape[1] // BLK)

    def store(cols, z):
        z_ref[:, cols] = z
        hidden_ref[:, cols] = (z / (1.0 + jnp.exp(-z))).astype(BF16)

    gather_sums(tab, prod, sums, store)


def output_body(order, tab, w_ref, *refs):
    pieces = len(order)
    out_ref, done_ref, ext, prod, *sums = refs[pieces:]
    done_ref[...] = jnp.zeros_like(done_ref)
    lay(ext, order, refs[:pieces])

    def store(cols, total):
        out_ref[:, cols] = total.astype(BF16)

    half = prod.shape[0] // 2
    for i in range(2):
        multiply(w_ref, ext[:, i * half * BLK : (i + 1) * half * BLK], prod, i * half)
    gather_sums(tab, prod, sums, store)


def halve_body(axis, keep_ref, got_ref, mine_ref, *send_refs):
    place = lax.axis_index(axis) // 2
    mine_ref[...] = keep_ref[place].astype(F32) + got_ref[place].astype(F32)
    for j, ref in enumerate(send_refs):
        other = place ^ (j + 1)
        ref[...] = (keep_ref[other].astype(F32) + got_ref[other].astype(F32)).astype(BF16)


def turn_body(count, tab, hidden_ref, mine_ref, *refs):
    gots, outs = refs[:count], refs[count:]
    rows = hidden_ref.shape[1]
    for i, (start, out_ref) in enumerate(zip(near_rim(tab), outs)):
        cols = slice(rows + i * RIM, rows + (i + 1) * RIM)
        total = mine_ref[:, cols]
        for ref in gots:
            total = total + ref[:, cols].astype(F32)
        out_ref[0] = total.astype(BF16)
        out_ref[1] = hidden_ref[:, pl.ds(start, RIM)]


def pack_body(hidden_ref, a_ref, b_ref, rim_ref, full_ref):
    rows = hidden_ref.shape[1]
    rim_ref[:, :RIM] = a_ref[1]
    rim_ref[:, RIM:] = b_ref[1]
    full_ref[:, :rows] = hidden_ref[...]
    full_ref[:, rows:] = rim_ref[...]


def append_body(wide_ref, rim_ref, full_ref):
    rows = wide_ref.shape[1]
    full_ref[:, :rows] = wide_ref[...]
    full_ref[:, rows:] = rim_ref[...]


def weight_grad(ext_ref, spread_ref, start, width):
    part = pl.ds(start, width)
    table = jnp.concatenate([spread_ref[s, part, :] for s in range(spread_ref.shape[0])], axis=1)
    res = lax.dot_general(ext_ref[...], table, (((1,), (1,)), ((), ())), preferred_element_type=F32)
    slabs = lax.axis_size("space")
    return res.reshape(slabs // 2, 2, res.shape[0] // slabs, width)


def part_slabs(ext_ref, spread_ref, keep_ref, send_ref, step):
    even = lax.axis_index("space") % 2 == 0

    def product(start, width):
        res = weight_grad(ext_ref, spread_ref, start, width)
        part = pl.ds(start, width)
        keep_ref[:, :, part] = jnp.where(even, res[:, 0], res[:, 1])
        send_ref[:, :, part] = jnp.where(even, res[:, 1], res[:, 0]).astype(BF16)

    chunks(keep_ref.shape[2], step, product)


def grad_two_body(order, spread_ref, *refs):
    pieces = len(order)
    keep_ref, send_ref, mine_ref, *send_refs, ext, total = refs[pieces:]
    lay(ext, order, refs[:pieces])
    cut = keep_ref.shape[2]
    part_slabs(ext, spread_ref, keep_ref, send_ref, cut)
    total[...] = weight_grad(ext, spread_ref, cut, mine_ref.shape[2])
    place = lax.axis_index("space") // 2
    mine_ref[...] = total[place]
    for j, ref in enumerate(send_refs):
        ref[...] = total[place ^ (j + 1)].astype(BF16)


def split_body(count, mine_ref, *refs):
    gots, (keep_ref, send_ref) = refs[:count], refs[count:]
    parity = lax.axis_index("space") % 2
    for ref, place in ((keep_ref, parity), (send_ref, 1 - parity)):
        total = mine_ref[place]
        for got in gots:
            total = total + got[place].astype(F32)
        ref[...] = total.astype(ref.dtype)


def prepare_body(z_ref, wide_ref, rims_ref, slope_ref, ext_ref):
    rows = wide_ref.shape[1]
    ext_ref[:, :rows] = wide_ref[...]
    ext_ref[:, rows:] = rims_ref[...]
    z = z_ref[...]
    gate = 1.0 / (1.0 + jnp.exp(-z))
    slope_ref[...] = gate * (1.0 + z * (1.0 - gate))


def grad_one_body(count, tab, slope_ref, from_a, from_b, ext_ref, mine_ref, *refs):
    gots, (keep_ref, send_ref, grads, blocks, spread_ref) = refs[:count], refs[count:]
    rows = slope_ref.shape[1]
    inner = mine_ref[:, :rows]
    for ref in gots:
        inner = inner + ref[:, :rows].astype(F32)
    grads[...] = inner
    a, b = near_rim(tab)
    for start, ref in ((a, from_a), (b, from_b)):
        grads[:, pl.ds(start, RIM)] = grads[:, pl.ds(start, RIM)] + ref[0].astype(F32)
    nblocks = blocks.shape[0] - 1
    for i in range(nblocks):
        cols = slice(i * BLK, (i + 1) * BLK)
        blocks[i] = (grads[:, cols] * slope_ref[:, cols]).astype(BF16).astype(F32)
    blocks[nblocks] = jnp.zeros_like(blocks[nblocks])
    spread(tab, blocks, spread_ref)
    part_slabs(ext_ref, spread_ref, keep_ref, send_ref, 7 * BLK)


def finish_body(counts, *refs):
    out_ref = refs[-1]
    depth = out_ref.shape[2]
    k = first = 0
    for count in counts:
        total = refs[first][...]
        for ref in refs[first + 1 : first + count]:
            total = total + ref[...].astype(F32)
        first += count
        for i in range(total.shape[1] // depth):
            out_ref[k] = total[:, i * depth : (i + 1) * depth]
            k += 1


def swap(value, axis, bits):
    return lax.ppermute(value, axis, [(i, i ^ bits) for i in range(lax.axis_size(axis))])


def swap_other(value):
    pairs = [(i, i + 1) for i in range(1, lax.axis_size("space") - 1, 2)]
    return lax.ppermute(value, "space", pairs + [(j, i) for i, j in pairs])


def local(features, kernel_map, block_count, weight_one, weight_two, cotangent):
    slabs, parts = lax.axis_size("space"), lax.axis_size("chan")
    pairs = parts // 2
    rows, depth = features.shape
    nblocks = rows // BLK
    reach = (nblocks + 2 * HB) * BLK
    offsets, entries = kernel_map.shape[1:3]
    wide = weight_one.shape[2]
    flat = offsets * depth
    share = wide // slabs
    order = [0, 1] + [v for j in range(1, pairs) for v in (2 * j, 2 * j + 1)]
    work = 2 * flat * wide * reach
    blocks = pltpu.VMEM((nblocks + 1, depth, BLK), F32)
    ext = pltpu.VMEM((wide, reach), BF16)
    spread_shape = (nblocks + 2 * HB, flat, BLK)

    def finish(*groups):
        total = call(
            functools.partial(finish_body, [len(g) for g in groups]),
            [jax.ShapeDtypeStruct((offsets, share, depth), F32)],
            [held(v) for g in groups for v in g],
            traffic=2 << 20,
        )[0]
        return total.transpose(0, 2, 1)

    def reduce_far(keep, got, after):
        width = keep.shape[2]
        mine, *sends = call(
            functools.partial(halve_body, "space"),
            [pltpu.VMEM((share, width), F32)] + [pltpu.VMEM((share, width), BF16)] * (slabs // 2 - 1),
            [held(keep), held(got)],
            traffic=2 << 20,
            after=after,
        )
        return [mine] + [swap(v, "space", 2 * (j + 1)) for j, v in enumerate(sends)]

    w_one = weight_one.reshape(flat, wide)
    w_two = weight_two.reshape(flat, wide)

    shard_t = features.T
    far = [swap(shard_t, "chan", 2 * j) for j in range(1, pairs)]
    cot = cotangent.T
    tab, spread_two, keep, send, own = call(
        input_grad_body,
        [
            pltpu.VMEM((entries + PAD, offsets), jnp.int32),
            pltpu.VMEM(spread_shape, BF16),
            pltpu.VMEM((pairs, depth, reach), BF16),
            pltpu.VMEM((pairs, depth, reach), BF16),
            pltpu.VMEM((depth, rows), BF16),
        ],
        [
            pltpu.with_memory_space_constraint(v, pltpu.HBM)
            for v in (block_count, kernel_map[0].transpose(2, 1, 0), cot, w_two, shard_t)
        ],
        [
            pltpu.VMEM((3, entries, offsets), jnp.int32),
            pltpu.VMEM(cot.shape, BF16),
            pltpu.VMEM(w_two.shape, BF16),
            blocks,
            pltpu.VMEM((parts, depth, reach), BF16),
            pltpu.SMEM((entries + PAD, offsets), jnp.int32),
            pltpu.SemaphoreType.DMA((4,)),
            pltpu.SemaphoreType.DMA,
        ],
        vmem=16,
        flops=work,
        traffic=16 << 20,
        specs=[SMEM] + [FAR] * 4,
    )
    pieces = [own, swap(shard_t, "chan", 1)]
    for got in far:
        (got,) = call(pass_body, [pltpu.VMEM(got.shape, BF16)], [held(got)], after=[send])
        pieces += [got, swap(got, "chan", 1)]
    half_rim = pltpu.VMEM((wide // 2, RIM), BF16)
    rim_a, rim_b = call(
        functools.partial(cut_body, order),
        [half_rim, half_rim],
        [tab] + [held(v) for v in pieces],
        [pltpu.VMEM((wide, RIM), BF16)],
        flops=8 * work,
    )
    x_a, x_b = swap(rim_a, "space", 1), swap_other(rim_b)
    got = swap(send, "chan", 1)
    mine, *sends = call(
        functools.partial(halve_body, "chan"),
        [pltpu.VMEM((depth, reach), F32)] + [pltpu.VMEM((depth, reach), BF16)] * (pairs - 1),
        [held(keep), held(got)],
        traffic=2 << 20,
        after=[rim_a],
    )
    gots = [swap(v, "chan", 2 * (j + 1)) for j, v in enumerate(sends)]

    conv_scratch = [ext, pltpu.VMEM(spread_shape, F32)] + [blocks] * 2
    prod_one, x_wide = call(
        functools.partial(inner_body, order),
        [pltpu.VMEM(spread_shape, F32), pltpu.VMEM((wide, rows), BF16)],
        [w_one] + [held(v) for v in pieces],
        vmem=10,
        flops=work,
        traffic=16 << 20,
        after=[mine],
    )
    (x_half,) = call(
        stack_body, [pltpu.VMEM((wide // 2, 2 * RIM), BF16)], [held(x_a), held(x_b)], after=[x_wide]
    )
    z_one, hidden, x_rims, _ = call(
        hidden_body,
        [pltpu.VMEM((depth, rows), F32), pltpu.VMEM((depth, rows), BF16), pltpu.VMEM((wide, 2 * RIM), BF16), pltpu.VMEM(spread_shape, F32)],
        [tab, w_one] + [held(v) for v in (x_half, swap(x_half, "chan", 1), prod_one)],
        [blocks] * 2,
        vmem=12,
        aliases={4: 3},
    )
    far = [swap(hidden, "chan", 2 * j) for j in range(1, pairs)]
    to_a, to_b = call(
        functools.partial(turn_body, len(gots)),
        [pltpu.VMEM((2, depth, RIM), BF16), pltpu.VMEM((2, depth, RIM), BF16)],
        [tab] + [held(v) for v in [hidden, mine] + gots],
        traffic=2 << 20,
    )
    from_a, from_b = swap(to_a, "space", 1), swap_other(to_b)
    rim, full = call(
        pack_body,
        [pltpu.VMEM((depth, 2 * RIM), BF16), pltpu.VMEM((depth, reach), BF16)],
        [held(v) for v in (hidden, from_a, from_b)],
        traffic=1 << 20,
    )
    far_rims = [swap(rim, "chan", 2 * j) for j in range(1, pairs)]
    full_other = swap(full, "chan", 1)

    slope, x_ext = call(
        prepare_body,
        [pltpu.VMEM((depth, rows), F32), pltpu.VMEM((wide, reach), BF16)],
        [held(v) for v in (z_one, x_wide, x_rims)],
        after=[to_a],
    )
    keep_one, send_one = call(
        functools.partial(grad_one_body, len(gots)),
        [pltpu.VMEM((slabs // 2, share, flat), F32), pltpu.VMEM((slabs // 2, share, flat), BF16)],
        [tab] + [held(v) for v in [slope, from_a, from_b, x_ext, mine] + gots],
        [pltpu.VMEM((depth, rows), F32), blocks, pltpu.VMEM(spread_shape, BF16)],
        vmem=24,
        flops=work,
        traffic=16 << 20,
    )
    got_one = swap(send_one, "space", 1)

    pieces = [full, full_other]
    for got, got_rim in zip(far, far_rims):
        (got,) = call(
            append_body, [pltpu.VMEM((depth, reach), BF16)], [held(got), held(got_rim)], traffic=1 << 20, after=[keep_one]
        )
        pieces += [got, swap(got, "chan", 1)]
    cut = min(Y_FIRST, offsets) * depth
    far_part = (2, share, flat - cut)
    keep_two, send_two, mine_far, *sends_far = call(
        functools.partial(grad_two_body, order),
        [
            pltpu.VMEM((slabs // 2, share, cut), F32),
            pltpu.VMEM((slabs // 2, share, cut), BF16),
            pltpu.VMEM(far_part, F32),
        ]
        + [pltpu.VMEM(far_part, BF16)] * (slabs // 2 - 1),
        [held(v) for v in [spread_two] + pieces],
        [ext, pltpu.VMEM((slabs // 2,) + far_part, F32)],
        vmem=14,
        flops=work // 4,
    )
    gots_far = [swap(v, "space", 2 * (j + 1)) for j, v in enumerate(sends_far)]
    got_two = swap(send_two, "space", 1)
    group_one = reduce_far(keep_one, got_one, [])
    output, done = call(
        functools.partial(output_body, order),
        [jax.ShapeDtypeStruct((depth, rows), BF16), pltpu.VMEM((8, BLK), F32)],
        [tab, w_two] + [held(v) for v in pieces],
        conv_scratch,
        vmem=34,
        flops=8 * work,
        traffic=16 << 20,
        after=[group_one[0]],
    )
    keep_far, send_far = call(
        functools.partial(split_body, len(gots_far)),
        [pltpu.VMEM(far_part[1:], F32), pltpu.VMEM(far_part[1:], BF16)],
        [held(v) for v in [mine_far] + gots_far],
        traffic=1 << 20,
        after=[done],
    )
    got_far = swap(send_far, "space", 1)
    group_two = reduce_far(keep_two, got_two, [keep_far])
    grad_one = finish(group_one)
    grad_two = finish(group_two, [keep_far, got_far])
    return output.T, grad_one, grad_two


def solution(mesh):
    return jax.shard_map(
        local,
        mesh=mesh,
        in_specs=(
            P("space", "chan"),
            P("space", None, None, None),
            P(),
            P(None, "chan", None),
            P(None, "chan", None),
            P("space", "chan"),
        ),
        out_specs=(P("space", "chan"), P(None, "chan", "space"), P(None, "chan", "space")),
        check_vma=False,
    )
```

```python
import functools

import jax
import jax.numpy as jnp
from jax import lax
from jax.experimental import pallas as pl
from jax.experimental.pallas import tpu as pltpu
from jax.sharding import PartitionSpec as P

BLK = 128
HB = 2
Y_FIRST = 24
RIM = HB * BLK
STEP = 256
F32 = jnp.float32
BF16 = jnp.bfloat16

VMEM = pl.BlockSpec(memory_space=pltpu.VMEM)
SMEM = pl.BlockSpec(memory_space=pltpu.SMEM)
FAR = pl.BlockSpec(memory_space=pltpu.HBM)
PAD = 8


def held(value):
    return pltpu.with_memory_space_constraint(value, pltpu.VMEM)


def call(body, outs, ins, scratch=(), flops=0, traffic=0, vmem=6, specs=None, after=(), aliases=None):
    specs = list(specs or [VMEM] * len(ins))
    first, last = len(ins), len(ins) + len(after)
    ins = list(ins) + [held(v) for v in after]
    specs += [VMEM] * len(after)

    def ordered(*refs):
        body(*refs[:first], *refs[last:])

    name = getattr(body, "func", body).__name__
    kernel = pl.pallas_call(
        ordered,
        out_shape=outs,
        in_specs=specs,
        out_specs=[VMEM] * len(outs),
        scratch_shapes=list(scratch),
        input_output_aliases=aliases or {},
        compiler_params=pltpu.CompilerParams(vmem_limit_bytes=vmem << 20),
        cost_estimate=pl.CostEstimate(flops=flops, bytes_accessed=traffic, transcendentals=0),
    )
    with jax.named_scope(name):
        return kernel(*ins)


def chunks(total, step, body):
    whole = total // step

    def one(i, _):
        body(pl.multiple_of(i * step, step), step)
        return 0

    lax.fori_loop(0, whole, one, 0)
    if total % step:
        body(whole * step, total % step)


def cell(code):
    return code >> 6, code & 63


def near_rim(tab):
    row = tab.shape[0] - PAD
    return pl.multiple_of(tab[row, 0], BLK), pl.multiple_of(tab[row, 1], BLK)


def held_rim(tab_ref):
    row = tab_ref.shape[0] - PAD
    return tuple(pl.multiple_of(jnp.max(tab_ref[row:, i : i + 1]), BLK) for i in range(2))


def table(counts, map_ref, nblocks):
    shard = lax.axis_index("space")
    even = shard % 2 == 0
    own_count, left_count = counts[shard], counts[jnp.maximum(shard - 1, 0)]
    source, inblock, target = map_ref[0], map_ref[1], map_ref[2]
    left = jnp.where(even, nblocks + HB, nblocks) - (left_count - HB)
    right = jnp.where(even, nblocks, nblocks + HB)
    position = inblock + jnp.where(source == shard, 0, jnp.where(source < shard, left, right))
    code = position * 64 + jnp.where(target < own_count, target, nblocks)
    entries = code.shape[0]
    index = lax.broadcasted_iota(jnp.int32, code.shape, 0)
    rank = jnp.zeros_like(code)
    for e in range(entries):
        row = code[e : e + 1]
        rank += ((row < code) | ((row == code) & (e < index))).astype(jnp.int32)
    rows = [jnp.sum(jnp.where(rank == e, code, 0), axis=0, keepdims=True) for e in range(entries)]
    tail = (own_count - HB) * BLK
    spot = (lax.broadcasted_iota(jnp.int32, (PAD, code.shape[1]), 1) == 0) == even
    return jnp.concatenate(rows + [jnp.where(spot, tail, 0)], axis=0)


def spread(tab, blocks, spread_ref):
    depth = blocks.shape[1]
    entries, offsets = tab.shape[0] - PAD, tab.shape[1]

    def one(k):
        rows = slice(k * depth, (k + 1) * depth)
        spread_ref[:, rows, :] = jnp.zeros((spread_ref.shape[0], depth, BLK), BF16)
        before, acc = -1, jnp.zeros((depth, BLK), F32)
        for e in range(entries):
            s, t = cell(tab[e, k])
            acc = jnp.where(s == before, acc, 0.0) + blocks[t]
            spread_ref[s, rows, :] = acc.astype(BF16)
            before = s

    for k in range(offsets):
        one(k)


def collect(tab, prod, sums):
    depth = sums[0].shape[1]
    entries, offsets = tab.shape[0] - PAD, tab.shape[1]
    for acc in sums:
        acc[...] = jnp.zeros_like(acc)

    def one(k, _):
        rows = pl.ds(pl.multiple_of(k * depth, depth), depth)
        for e in range(entries):
            acc = sums[e % len(sums)]
            s, t = cell(tab[e, k])
            acc[t] = acc[t] + prod[s, rows, :]
        return 0

    lax.fori_loop(0, offsets, one, 0)


def lay(ext_ref, order, refs):
    depth = refs[0].shape[0]
    for bits, ref in zip(order, refs):
        place = lax.axis_index("chan") ^ bits
        ext_ref[pl.ds(pl.multiple_of(place * depth, depth), depth), :] = ref[...]


def input_grad_body(
    counts, map_hbm, cot_hbm, w_hbm, feat_hbm, tab_ref, spread_ref, keep_ref, send_ref,
    own_ref, map_ref, cot_ref, w_ref, blocks, part, tab, sems, sem
):
    ways = [(map_hbm, map_ref), (cot_hbm, cot_ref), (w_hbm, w_ref), (feat_hbm, own_ref)]
    loads = [pltpu.make_async_copy(src, dst, sems.at[i]) for i, (src, dst) in enumerate(ways)]
    for load in loads:
        load.start()
    depth, rows = cot_ref.shape
    nblocks = rows // BLK
    loads[0].wait()
    tab_ref[...] = table(counts, map_ref, nblocks)
    copy = pltpu.make_async_copy(tab_ref, tab, sem)
    copy.start()
    loads[1].wait()
    for b in range(nblocks):
        blocks[b] = cot_ref[:, b * BLK : (b + 1) * BLK].astype(F32)
    blocks[nblocks] = jnp.zeros_like(blocks[nblocks])
    copy.wait()
    spread(tab, blocks, spread_ref)
    loads[2].wait()

    half = spread_ref.shape[0] // 2

    def product(i, _):
        table = jnp.concatenate([spread_ref[i * half + j] for j in range(half)], axis=1)
        res = lax.dot_general(w_ref[...], table, (((0,), (0,)), ((), ())), preferred_element_type=F32)
        cols = pl.ds(pl.multiple_of(i * half * BLK, BLK), half * BLK)
        part[:, :, cols] = res.astype(BF16).reshape(part.shape[0], depth, half * BLK)
        return 0

    lax.fori_loop(0, 2, product, 0)
    core = lax.axis_index("chan") % 2
    for j in range(keep_ref.shape[0]):
        keep_ref[j] = part[2 * j + core]
        send_ref[j] = part[2 * j + 1 - core]
    loads[3].wait()


def pass_body(value_ref, out_ref):
    out_ref[...] = value_ref[...]


def cut_body(order, tab, *refs):
    pieces = len(order)
    a_ref, b_ref, rims = refs[pieces:]
    depth, half = refs[0].shape[0], a_ref.shape[0]
    own = pl.ds(pl.multiple_of(lax.axis_index("chan") % 2 * half, half), half)
    for start, out_ref in zip(held_rim(tab), (a_ref, b_ref)):
        for bits, ref in zip(order, refs[:pieces]):
            place = lax.axis_index("chan") ^ bits
            rims[pl.ds(pl.multiple_of(place * depth, depth), depth), :] = ref[:, pl.ds(start, RIM)]
        out_ref[...] = rims[own, :]


def multiply(w_ref, value, prod, first):
    res = jnp.dot(w_ref[...], value, preferred_element_type=F32)
    for j in range(value.shape[1] // BLK):
        prod[first + j] = res[:, j * BLK : (j + 1) * BLK]


def gather_sums(tab, prod, sums, store):
    collect(tab, prod, sums)
    for b in range(sums[0].shape[0] - 1):
        total = sums[0][b]
        for acc in sums[1:]:
            total = total + acc[b]
        store(slice(b * BLK, (b + 1) * BLK), total)


def inner_body(order, w_ref, *refs):
    pieces = len(order)
    prod_ref, wide_ref = refs[pieces:]
    lay(wide_ref, order, refs[:pieces])
    multiply(w_ref, wide_ref[...], prod_ref, 0)


def stack_body(a_ref, b_ref, out_ref):
    out_ref[:, :RIM] = a_ref[...]
    out_ref[:, RIM:] = b_ref[...]


def hidden_body(tab_ref, w_ref, own_ref, other_ref, _, z_ref, hidden_ref, rims_ref, prod, tab, sem, *sums):
    fetch = pltpu.make_async_copy(tab_ref, tab, sem)
    fetch.start()
    core, half = lax.axis_index("chan") % 2, own_ref.shape[0]
    for place, ref in ((core, own_ref), (1 - core, other_ref)):
        rims_ref[pl.ds(pl.multiple_of(place * half, half), half), :] = ref[...]
    multiply(w_ref, rims_ref[...], prod, z_ref.shape[1] // BLK)
    fetch.wait()

    def store(cols, z):
        z_ref[:, cols] = z
        hidden_ref[:, cols] = (z / (1.0 + jnp.exp(-z))).astype(BF16)

    gather_sums(tab, prod, sums, store)


def output_body(order, tab_ref, w_ref, *refs):
    pieces = len(order)
    out_ref, done_ref, ext, prod, tab, sem, *sums = refs[pieces:]
    fetch = pltpu.make_async_copy(tab_ref, tab, sem)
    fetch.start()
    done_ref[...] = jnp.zeros_like(done_ref)
    lay(ext, order, refs[:pieces])

    def store(cols, total):
        out_ref[:, cols] = total.astype(BF16)

    half = prod.shape[0] // 2
    for i in range(2):
        multiply(w_ref, ext[:, i * half * BLK : (i + 1) * half * BLK], prod, i * half)
    fetch.wait()
    gather_sums(tab, prod, sums, store)


def halve_body(axis, keep_ref, got_ref, mine_ref, *send_refs):
    place = lax.axis_index(axis) // 2
    mine_ref[...] = keep_ref[place].astype(F32) + got_ref[place].astype(F32)
    for j, ref in enumerate(send_refs):
        other = place ^ (j + 1)
        ref[...] = (keep_ref[other].astype(F32) + got_ref[other].astype(F32)).astype(BF16)


def turn_body(count, tab, hidden_ref, mine_ref, *refs):
    gots, outs = refs[:count], refs[count:]
    rows = hidden_ref.shape[1]
    for i, (start, out_ref) in enumerate(zip(held_rim(tab), outs)):
        cols = slice(rows + i * RIM, rows + (i + 1) * RIM)
        total = mine_ref[:, cols]
        for ref in gots:
            total = total + ref[:, cols].astype(F32)
        out_ref[0] = total.astype(BF16)
        out_ref[1] = hidden_ref[:, pl.ds(start, RIM)]


def pack_body(hidden_ref, a_ref, b_ref, rim_ref, full_ref):
    rows = hidden_ref.shape[1]
    rim_ref[:, :RIM] = a_ref[1]
    rim_ref[:, RIM:] = b_ref[1]
    full_ref[:, :rows] = hidden_ref[...]
    full_ref[:, rows:] = rim_ref[...]


def append_body(wide_ref, rim_ref, full_ref):
    rows = wide_ref.shape[1]
    full_ref[:, :rows] = wide_ref[...]
    full_ref[:, rows:] = rim_ref[...]


def weight_grad(ext_ref, spread_ref, start, width):
    part = pl.ds(start, width)
    table = jnp.concatenate([spread_ref[s, part, :] for s in range(spread_ref.shape[0])], axis=1)
    res = lax.dot_general(ext_ref[...], table, (((1,), (1,)), ((), ())), preferred_element_type=F32)
    slabs = lax.axis_size("space")
    return res.reshape(slabs // 2, 2, res.shape[0] // slabs, width)


def part_slabs(ext_ref, spread_ref, keep_ref, send_ref, step):
    even = lax.axis_index("space") % 2 == 0

    def product(start, width):
        res = weight_grad(ext_ref, spread_ref, start, width)
        part = pl.ds(start, width)
        keep_ref[:, :, part] = jnp.where(even, res[:, 0], res[:, 1])
        send_ref[:, :, part] = jnp.where(even, res[:, 1], res[:, 0]).astype(BF16)

    chunks(keep_ref.shape[2], step, product)


def grad_two_body(order, spread_ref, *refs):
    pieces = len(order)
    keep_ref, send_ref, mine_ref, *send_refs, ext, total = refs[pieces:]
    lay(ext, order, refs[:pieces])
    cut = keep_ref.shape[2]
    part_slabs(ext, spread_ref, keep_ref, send_ref, cut)
    total[...] = weight_grad(ext, spread_ref, cut, mine_ref.shape[2])
    place = lax.axis_index("space") // 2
    mine_ref[...] = total[place]
    for j, ref in enumerate(send_refs):
        ref[...] = total[place ^ (j + 1)].astype(BF16)


def split_body(count, mine_ref, *refs):
    gots, (keep_ref, send_ref) = refs[:count], refs[count:]
    parity = lax.axis_index("space") % 2
    for ref, place in ((keep_ref, parity), (send_ref, 1 - parity)):
        total = mine_ref[place]
        for got in gots:
            total = total + got[place].astype(F32)
        ref[...] = total.astype(ref.dtype)


def prepare_body(z_ref, wide_ref, rims_ref, slope_ref, ext_ref):
    rows = wide_ref.shape[1]
    ext_ref[:, :rows] = wide_ref[...]
    ext_ref[:, rows:] = rims_ref[...]
    z = z_ref[...]
    gate = 1.0 / (1.0 + jnp.exp(-z))
    slope_ref[...] = gate * (1.0 + z * (1.0 - gate))


def grad_one_body(count, tab_ref, slope_ref, from_a, from_b, ext_ref, mine_ref, *refs):
    gots, (keep_ref, send_ref, grads, blocks, spread_ref, tab, sem) = refs[:count], refs[count:]
    fetch = pltpu.make_async_copy(tab_ref, tab, sem)
    fetch.start()
    rows = slope_ref.shape[1]
    inner = mine_ref[:, :rows]
    for ref in gots:
        inner = inner + ref[:, :rows].astype(F32)
    grads[...] = inner
    fetch.wait()
    a, b = near_rim(tab)
    for start, ref in ((a, from_a), (b, from_b)):
        grads[:, pl.ds(start, RIM)] = grads[:, pl.ds(start, RIM)] + ref[0].astype(F32)
    nblocks = blocks.shape[0] - 1
    for i in range(nblocks):
        cols = slice(i * BLK, (i + 1) * BLK)
        blocks[i] = (grads[:, cols] * slope_ref[:, cols]).astype(BF16).astype(F32)
    blocks[nblocks] = jnp.zeros_like(blocks[nblocks])
    spread(tab, blocks, spread_ref)
    part_slabs(ext_ref, spread_ref, keep_ref, send_ref, 7 * BLK)


def finish_body(counts, *refs):
    out_ref = refs[-1]
    depth = out_ref.shape[2]
    k = first = 0
    for count in counts:
        total = refs[first][...]
        for ref in refs[first + 1 : first + count]:
            total = total + ref[...].astype(F32)
        first += count
        for i in range(total.shape[1] // depth):
            out_ref[k] = total[:, i * depth : (i + 1) * depth]
            k += 1


def swap(value, axis, bits):
    return lax.ppermute(value, axis, [(i, i ^ bits) for i in range(lax.axis_size(axis))])


def swap_other(value):
    pairs = [(i, i + 1) for i in range(1, lax.axis_size("space") - 1, 2)]
    return lax.ppermute(value, "space", pairs + [(j, i) for i, j in pairs])


def local(features, kernel_map, block_count, weight_one, weight_two, cotangent):
    slabs, parts = lax.axis_size("space"), lax.axis_size("chan")
    pairs = parts // 2
    rows, depth = features.shape
    nblocks = rows // BLK
    reach = (nblocks + 2 * HB) * BLK
    offsets, entries = kernel_map.shape[1:3]
    wide = weight_one.shape[2]
    flat = offsets * depth
    share = wide // slabs
    order = [0, 1] + [v for j in range(1, pairs) for v in (2 * j, 2 * j + 1)]
    work = 2 * flat * wide * reach
    blocks = pltpu.VMEM((nblocks + 1, depth, BLK), F32)
    ext = pltpu.VMEM((wide, reach), BF16)
    spread_shape = (nblocks + 2 * HB, flat, BLK)

    def finish(*groups):
        total = call(
            functools.partial(finish_body, [len(g) for g in groups]),
            [jax.ShapeDtypeStruct((offsets, share, depth), F32)],
            [held(v) for g in groups for v in g],
            traffic=2 << 20,
        )[0]
        return total.transpose(0, 2, 1)

    def reduce_far(keep, got, after):
        width = keep.shape[2]
        mine, *sends = call(
            functools.partial(halve_body, "space"),
            [pltpu.VMEM((share, width), F32)] + [pltpu.VMEM((share, width), BF16)] * (slabs // 2 - 1),
            [held(keep), held(got)],
            traffic=2 << 20,
            after=after,
        )
        return [mine] + [swap(v, "space", 2 * (j + 1)) for j, v in enumerate(sends)]

    w_one = weight_one.reshape(flat, wide)
    w_two = weight_two.reshape(flat, wide)

    shard_t = features.T
    far = [swap(shard_t, "chan", 2 * j) for j in range(1, pairs)]
    cot = cotangent.T
    tab, spread_two, keep, send, own = call(
        input_grad_body,
        [
            pltpu.VMEM((entries + PAD, offsets), jnp.int32),
            pltpu.VMEM(spread_shape, BF16),
            pltpu.VMEM((pairs, depth, reach), BF16),
            pltpu.VMEM((pairs, depth, reach), BF16),
            pltpu.VMEM((depth, rows), BF16),
        ],
        [
            pltpu.with_memory_space_constraint(v, pltpu.HBM)
            for v in (block_count, kernel_map[0].transpose(2, 1, 0), cot, w_two, shard_t)
        ],
        [
            pltpu.VMEM((3, entries, offsets), jnp.int32),
            pltpu.VMEM(cot.shape, BF16),
            pltpu.VMEM(w_two.shape, BF16),
            blocks,
            pltpu.VMEM((parts, depth, reach), BF16),
            pltpu.SMEM((entries + PAD, offsets), jnp.int32),
            pltpu.SemaphoreType.DMA((4,)),
            pltpu.SemaphoreType.DMA,
        ],
        vmem=16,
        flops=work,
        traffic=16 << 20,
        specs=[SMEM] + [FAR] * 4,
    )
    pieces = [own, swap(shard_t, "chan", 1)]
    for got in far:
        (got,) = call(pass_body, [pltpu.VMEM(got.shape, BF16)], [held(got)], after=[send])
        pieces += [got, swap(got, "chan", 1)]
    half_rim = pltpu.VMEM((wide // 2, RIM), BF16)
    rim_a, rim_b = call(
        functools.partial(cut_body, order),
        [half_rim, half_rim],
        [held(tab)] + [held(v) for v in pieces],
        [pltpu.VMEM((wide, RIM), BF16)],
        flops=8 * work,
    )
    x_a, x_b = swap(rim_a, "space", 1), swap_other(rim_b)
    got = swap(send, "chan", 1)
    mine, *sends = call(
        functools.partial(halve_body, "chan"),
        [pltpu.VMEM((depth, reach), F32)] + [pltpu.VMEM((depth, reach), BF16)] * (pairs - 1),
        [held(keep), held(got)],
        traffic=2 << 20,
        after=[rim_a],
    )
    gots = [swap(v, "chan", 2 * (j + 1)) for j, v in enumerate(sends)]

    table_scratch = [pltpu.SMEM((entries + PAD, offsets), jnp.int32), pltpu.SemaphoreType.DMA]
    conv_scratch = [ext, pltpu.VMEM(spread_shape, F32)] + table_scratch + [blocks] * 2
    prod_one, x_wide = call(
        functools.partial(inner_body, order),
        [pltpu.VMEM(spread_shape, F32), pltpu.VMEM((wide, rows), BF16)],
        [w_one] + [held(v) for v in pieces],
        vmem=10,
        flops=work,
        traffic=16 << 20,
        after=[mine],
    )
    (x_half,) = call(
        stack_body, [pltpu.VMEM((wide // 2, 2 * RIM), BF16)], [held(x_a), held(x_b)], after=[x_wide]
    )
    z_one, hidden, x_rims, _ = call(
        hidden_body,
        [pltpu.VMEM((depth, rows), F32), pltpu.VMEM((depth, rows), BF16), pltpu.VMEM((wide, 2 * RIM), BF16), pltpu.VMEM(spread_shape, F32)],
        [held(tab), w_one] + [held(v) for v in (x_half, swap(x_half, "chan", 1), prod_one)],
        table_scratch + [blocks] * 2,
        vmem=12,
        aliases={4: 3},
    )
    far = [swap(hidden, "chan", 2 * j) for j in range(1, pairs)]
    to_a, to_b = call(
        functools.partial(turn_body, len(gots)),
        [pltpu.VMEM((2, depth, RIM), BF16), pltpu.VMEM((2, depth, RIM), BF16)],
        [held(tab)] + [held(v) for v in [hidden, mine] + gots],
        traffic=2 << 20,
    )
    from_a, from_b = swap(to_a, "space", 1), swap_other(to_b)
    rim, full = call(
        pack_body,
        [pltpu.VMEM((depth, 2 * RIM), BF16), pltpu.VMEM((depth, reach), BF16)],
        [held(v) for v in (hidden, from_a, from_b)],
        traffic=1 << 20,
    )
    far_rims = [swap(rim, "chan", 2 * j) for j in range(1, pairs)]
    full_other = swap(full, "chan", 1)

    slope, x_ext = call(
        prepare_body,
        [pltpu.VMEM((depth, rows), F32), pltpu.VMEM((wide, reach), BF16)],
        [held(v) for v in (z_one, x_wide, x_rims)],
        after=[to_a],
    )
    keep_one, send_one = call(
        functools.partial(grad_one_body, len(gots)),
        [pltpu.VMEM((slabs // 2, share, flat), F32), pltpu.VMEM((slabs // 2, share, flat), BF16)],
        [held(tab)] + [held(v) for v in [slope, from_a, from_b, x_ext, mine] + gots],
        [pltpu.VMEM((depth, rows), F32), blocks, pltpu.VMEM(spread_shape, BF16)] + table_scratch,
        vmem=24,
        flops=work,
        traffic=16 << 20,
    )
    got_one = swap(send_one, "space", 1)

    pieces = [full, full_other]
    for got, got_rim in zip(far, far_rims):
        (got,) = call(
            append_body, [pltpu.VMEM((depth, reach), BF16)], [held(got), held(got_rim)], traffic=1 << 20, after=[keep_one]
        )
        pieces += [got, swap(got, "chan", 1)]
    cut = min(Y_FIRST, offsets) * depth
    far_part = (2, share, flat - cut)
    keep_two, send_two, mine_far, *sends_far = call(
        functools.partial(grad_two_body, order),
        [
            pltpu.VMEM((slabs // 2, share, cut), F32),
            pltpu.VMEM((slabs // 2, share, cut), BF16),
            pltpu.VMEM(far_part, F32),
        ]
        + [pltpu.VMEM(far_part, BF16)] * (slabs // 2 - 1),
        [held(v) for v in [spread_two] + pieces],
        [ext, pltpu.VMEM((slabs // 2,) + far_part, F32)],
        vmem=14,
        flops=work // 4,
    )
    gots_far = [swap(v, "space", 2 * (j + 1)) for j, v in enumerate(sends_far)]
    got_two = swap(send_two, "space", 1)
    group_one = reduce_far(keep_one, got_one, [])
    output, done = call(
        functools.partial(output_body, order),
        [jax.ShapeDtypeStruct((depth, rows), BF16), pltpu.VMEM((8, BLK), F32)],
        [held(tab), w_two] + [held(v) for v in pieces],
        conv_scratch,
        vmem=34,
        flops=8 * work,
        traffic=16 << 20,
        after=[group_one[0]],
    )
    keep_far, send_far = call(
        functools.partial(split_body, len(gots_far)),
        [pltpu.VMEM(far_part[1:], F32), pltpu.VMEM(far_part[1:], BF16)],
        [held(v) for v in [mine_far] + gots_far],
        traffic=1 << 20,
        after=[done],
    )
    got_far = swap(send_far, "space", 1)
    group_two = reduce_far(keep_two, got_two, [keep_far])
    grad_one = finish(group_one)
    grad_two = finish(group_two, [keep_far, got_far])
    return output.T, grad_one, grad_two


def solution(mesh):
    return jax.shard_map(
        local,
        mesh=mesh,
        in_specs=(
            P("space", "chan"),
            P("space", None, None, None),
            P(),
            P(None, "chan", None),
            P(None, "chan", None),
            P("space", "chan"),
        ),
        out_specs=(P("space", "chan"), P(None, "chan", "space"), P(None, "chan", "space")),
        check_vma=False,
    )
```

```python
import functools

import jax
import jax.numpy as jnp
from jax import lax
from jax.experimental import pallas as pl
from jax.experimental.pallas import tpu as pltpu
from jax.sharding import PartitionSpec as P

BLK = 128
HB = 2
Y_FIRST = 24
RIM = HB * BLK
STEP = 256
F32 = jnp.float32
BF16 = jnp.bfloat16

VMEM = pl.BlockSpec(memory_space=pltpu.VMEM)
SMEM = pl.BlockSpec(memory_space=pltpu.SMEM)
FAR = pl.BlockSpec(memory_space=pltpu.HBM)
PAD = 8


def held(value):
    return pltpu.with_memory_space_constraint(value, pltpu.VMEM)


def call(body, outs, ins, scratch=(), flops=0, traffic=0, vmem=6, specs=None, after=(), aliases=None):
    specs = list(specs or [VMEM] * len(ins))
    first, last = len(ins), len(ins) + len(after)
    ins = list(ins) + [held(v) for v in after]
    specs += [VMEM] * len(after)

    def ordered(*refs):
        body(*refs[:first], *refs[last:])

    name = getattr(body, "func", body).__name__
    kernel = pl.pallas_call(
        ordered,
        out_shape=outs,
        in_specs=specs,
        out_specs=[VMEM] * len(outs),
        scratch_shapes=list(scratch),
        input_output_aliases=aliases or {},
        compiler_params=pltpu.CompilerParams(vmem_limit_bytes=vmem << 20),
        cost_estimate=pl.CostEstimate(flops=flops, bytes_accessed=traffic, transcendentals=0),
    )
    with jax.named_scope(name):
        return kernel(*ins)


def chunks(total, step, body):
    whole = total // step

    def one(i, _):
        body(pl.multiple_of(i * step, step), step)
        return 0

    lax.fori_loop(0, whole, one, 0)
    if total % step:
        body(whole * step, total % step)


def cell(code):
    return code >> 6, code & 63


def near_rim(tab):
    row = tab.shape[0] - PAD
    return pl.multiple_of(tab[row, 0], BLK), pl.multiple_of(tab[row, 1], BLK)


def held_rim(tab_ref):
    row = tab_ref.shape[0] - PAD
    return tuple(pl.multiple_of(jnp.max(tab_ref[row:, i : i + 1]), BLK) for i in range(2))


def table(counts, map_ref, nblocks):
    shard = lax.axis_index("space")
    even = shard % 2 == 0
    own_count, left_count = counts[shard], counts[jnp.maximum(shard - 1, 0)]
    source, inblock, target = map_ref[0], map_ref[1], map_ref[2]
    left = jnp.where(even, nblocks + HB, nblocks) - (left_count - HB)
    right = jnp.where(even, nblocks, nblocks + HB)
    position = inblock + jnp.where(source == shard, 0, jnp.where(source < shard, left, right))
    code = position * 64 + jnp.where(target < own_count, target, nblocks)
    entries = code.shape[0]
    index = lax.broadcasted_iota(jnp.int32, code.shape, 0)
    rank = jnp.zeros_like(code)
    for e in range(entries):
        row = code[e : e + 1]
        rank += ((row < code) | ((row == code) & (e < index))).astype(jnp.int32)
    rows = [jnp.sum(jnp.where(rank == e, code, 0), axis=0, keepdims=True) for e in range(entries)]
    tail = (own_count - HB) * BLK
    spot = (lax.broadcasted_iota(jnp.int32, (PAD, code.shape[1]), 1) == 0) == even
    return jnp.concatenate(rows + [jnp.where(spot, tail, 0)], axis=0)


def spread(tab, blocks, spread_ref):
    depth = blocks.shape[1]
    entries, offsets = tab.shape[0] - PAD, tab.shape[1]

    def one(k):
        rows = slice(k * depth, (k + 1) * depth)
        spread_ref[:, rows, :] = jnp.zeros((spread_ref.shape[0], depth, BLK), BF16)
        before, acc = -1, jnp.zeros((depth, BLK), F32)
        for e in range(entries):
            s, t = cell(tab[e, k])
            acc = jnp.where(s == before, acc, 0.0) + blocks[t]
            spread_ref[s, rows, :] = acc.astype(BF16)
            before = s

    for k in range(offsets):
        one(k)


def collect(tab, prod, sums):
    depth = sums[0].shape[1]
    entries, offsets = tab.shape[0] - PAD, tab.shape[1]
    for acc in sums:
        acc[...] = jnp.zeros_like(acc)

    def one(k, _):
        rows = pl.ds(pl.multiple_of(k * depth, depth), depth)
        for e in range(entries):
            acc = sums[e % len(sums)]
            s, t = cell(tab[e, k])
            acc[t] = acc[t] + prod[s, rows, :]
        return 0

    lax.fori_loop(0, offsets, one, 0)


def lay(ext_ref, order, refs):
    depth = refs[0].shape[0]
    for bits, ref in zip(order, refs):
        place = lax.axis_index("chan") ^ bits
        ext_ref[pl.ds(pl.multiple_of(place * depth, depth), depth), :] = ref[...]


def input_grad_body(
    counts_hbm, map_hbm, cot_hbm, w_hbm, feat_hbm, tab_ref, spread_ref, keep_ref, send_ref,
    own_ref, map_ref, cot_ref, w_ref, blocks, part, tab, counts, sems, sem
):
    ways = [(map_hbm, map_ref), (cot_hbm, cot_ref), (w_hbm, w_ref), (feat_hbm, own_ref), (counts_hbm, counts)]
    loads = [pltpu.make_async_copy(src, dst, sems.at[i]) for i, (src, dst) in enumerate(ways)]
    for load in loads:
        load.start()
    depth, rows = cot_ref.shape
    nblocks = rows // BLK
    loads[0].wait()
    loads[4].wait()
    tab_ref[...] = table(counts, map_ref, nblocks)
    copy = pltpu.make_async_copy(tab_ref, tab, sem)
    copy.start()
    loads[1].wait()
    for b in range(nblocks):
        blocks[b] = cot_ref[:, b * BLK : (b + 1) * BLK].astype(F32)
    blocks[nblocks] = jnp.zeros_like(blocks[nblocks])
    copy.wait()
    spread(tab, blocks, spread_ref)
    loads[2].wait()

    half = spread_ref.shape[0] // 2

    def product(i, _):
        table = jnp.concatenate([spread_ref[i * half + j] for j in range(half)], axis=1)
        res = lax.dot_general(w_ref[...], table, (((0,), (0,)), ((), ())), preferred_element_type=F32)
        cols = pl.ds(pl.multiple_of(i * half * BLK, BLK), half * BLK)
        part[:, :, cols] = res.astype(BF16).reshape(part.shape[0], depth, half * BLK)
        return 0

    lax.fori_loop(0, 2, product, 0)
    core = lax.axis_index("chan") % 2
    for j in range(keep_ref.shape[0]):
        keep_ref[j] = part[2 * j + core]
        send_ref[j] = part[2 * j + 1 - core]
    loads[3].wait()


def pass_body(value_ref, out_ref):
    out_ref[...] = value_ref[...]


def cut_body(order, tab, *refs):
    pieces = len(order)
    a_ref, b_ref, rims = refs[pieces:]
    depth, half = refs[0].shape[0], a_ref.shape[0]
    own = pl.ds(pl.multiple_of(lax.axis_index("chan") % 2 * half, half), half)
    for start, out_ref in zip(held_rim(tab), (a_ref, b_ref)):
        for bits, ref in zip(order, refs[:pieces]):
            place = lax.axis_index("chan") ^ bits
            rims[pl.ds(pl.multiple_of(place * depth, depth), depth), :] = ref[:, pl.ds(start, RIM)]
        out_ref[...] = rims[own, :]


def multiply(w_ref, value, prod, first):
    res = jnp.dot(w_ref[...], value, preferred_element_type=F32)
    for j in range(value.shape[1] // BLK):
        prod[first + j] = res[:, j * BLK : (j + 1) * BLK]


def gather_sums(tab, prod, sums, store):
    collect(tab, prod, sums)
    for b in range(sums[0].shape[0] - 1):
        total = sums[0][b]
        for acc in sums[1:]:
            total = total + acc[b]
        store(slice(b * BLK, (b + 1) * BLK), total)


def inner_body(order, w_ref, *refs):
    pieces = len(order)
    prod_ref, wide_ref = refs[pieces:]
    lay(wide_ref, order, refs[:pieces])
    multiply(w_ref, wide_ref[...], prod_ref, 0)


def stack_body(a_ref, b_ref, out_ref):
    out_ref[:, :RIM] = a_ref[...]
    out_ref[:, RIM:] = b_ref[...]


def hidden_body(tab_ref, w_ref, own_ref, other_ref, _, z_ref, hidden_ref, rims_ref, prod, tab, sem, *sums):
    fetch = pltpu.make_async_copy(tab_ref, tab, sem)
    fetch.start()
    core, half = lax.axis_index("chan") % 2, own_ref.shape[0]
    for place, ref in ((core, own_ref), (1 - core, other_ref)):
        rims_ref[pl.ds(pl.multiple_of(place * half, half), half), :] = ref[...]
    multiply(w_ref, rims_ref[...], prod, z_ref.shape[1] // BLK)
    fetch.wait()

    def store(cols, z):
        z_ref[:, cols] = z
        hidden_ref[:, cols] = (z / (1.0 + jnp.exp(-z))).astype(BF16)

    gather_sums(tab, prod, sums, store)


def output_body(order, tab_ref, w_ref, *refs):
    pieces = len(order)
    out_ref, done_ref, ext, prod, tab, sem, *sums = refs[pieces:]
    fetch = pltpu.make_async_copy(tab_ref, tab, sem)
    fetch.start()
    done_ref[...] = jnp.zeros_like(done_ref)
    lay(ext, order, refs[:pieces])

    def store(cols, total):
        out_ref[:, cols] = total.astype(BF16)

    half = prod.shape[0] // 2
    for i in range(2):
        multiply(w_ref, ext[:, i * half * BLK : (i + 1) * half * BLK], prod, i * half)
    fetch.wait()
    gather_sums(tab, prod, sums, store)


def halve_body(axis, keep_ref, got_ref, mine_ref, *send_refs):
    place = lax.axis_index(axis) // 2
    mine_ref[...] = keep_ref[place].astype(F32) + got_ref[place].astype(F32)
    for j, ref in enumerate(send_refs):
        other = place ^ (j + 1)
        ref[...] = (keep_ref[other].astype(F32) + got_ref[other].astype(F32)).astype(BF16)


def turn_body(count, tab, hidden_ref, mine_ref, *refs):
    gots, outs = refs[:count], refs[count:]
    rows = hidden_ref.shape[1]
    for i, (start, out_ref) in enumerate(zip(held_rim(tab), outs)):
        cols = slice(rows + i * RIM, rows + (i + 1) * RIM)
        total = mine_ref[:, cols]
        for ref in gots:
            total = total + ref[:, cols].astype(F32)
        out_ref[0] = total.astype(BF16)
        out_ref[1] = hidden_ref[:, pl.ds(start, RIM)]


def pack_body(hidden_ref, a_ref, b_ref, rim_ref, full_ref):
    rows = hidden_ref.shape[1]
    rim_ref[:, :RIM] = a_ref[1]
    rim_ref[:, RIM:] = b_ref[1]
    full_ref[:, :rows] = hidden_ref[...]
    full_ref[:, rows:] = rim_ref[...]


def append_body(wide_ref, rim_ref, full_ref):
    rows = wide_ref.shape[1]
    full_ref[:, :rows] = wide_ref[...]
    full_ref[:, rows:] = rim_ref[...]


def weight_grad(ext_ref, spread_ref, start, width):
    part = pl.ds(start, width)
    table = jnp.concatenate([spread_ref[s, part, :] for s in range(spread_ref.shape[0])], axis=1)
    res = lax.dot_general(ext_ref[...], table, (((1,), (1,)), ((), ())), preferred_element_type=F32)
    slabs = lax.axis_size("space")
    return res.reshape(slabs // 2, 2, res.shape[0] // slabs, width)


def part_slabs(ext_ref, spread_ref, keep_ref, send_ref, step):
    even = lax.axis_index("space") % 2 == 0

    def product(start, width):
        res = weight_grad(ext_ref, spread_ref, start, width)
        part = pl.ds(start, width)
        keep_ref[:, :, part] = jnp.where(even, res[:, 0], res[:, 1])
        send_ref[:, :, part] = jnp.where(even, res[:, 1], res[:, 0]).astype(BF16)

    chunks(keep_ref.shape[2], step, product)


def grad_two_body(order, spread_ref, *refs):
    pieces = len(order)
    keep_ref, send_ref, mine_ref, *send_refs, ext, total = refs[pieces:]
    lay(ext, order, refs[:pieces])
    cut = keep_ref.shape[2]
    part_slabs(ext, spread_ref, keep_ref, send_ref, cut)
    total[...] = weight_grad(ext, spread_ref, cut, mine_ref.shape[2])
    place = lax.axis_index("space") // 2
    mine_ref[...] = total[place]
    for j, ref in enumerate(send_refs):
        ref[...] = total[place ^ (j + 1)].astype(BF16)


def split_body(count, mine_ref, *refs):
    gots, (keep_ref, send_ref) = refs[:count], refs[count:]
    parity = lax.axis_index("space") % 2
    for ref, place in ((keep_ref, parity), (send_ref, 1 - parity)):
        total = mine_ref[place]
        for got in gots:
            total = total + got[place].astype(F32)
        ref[...] = total.astype(ref.dtype)


def prepare_body(z_ref, wide_ref, rims_ref, slope_ref, ext_ref):
    rows = wide_ref.shape[1]
    ext_ref[:, :rows] = wide_ref[...]
    ext_ref[:, rows:] = rims_ref[...]
    z = z_ref[...]
    gate = 1.0 / (1.0 + jnp.exp(-z))
    slope_ref[...] = gate * (1.0 + z * (1.0 - gate))


def grad_one_body(count, tab_ref, slope_ref, from_a, from_b, ext_ref, mine_ref, *refs):
    gots, (keep_ref, send_ref, grads, blocks, spread_ref, tab, sem) = refs[:count], refs[count:]
    fetch = pltpu.make_async_copy(tab_ref, tab, sem)
    fetch.start()
    rows = slope_ref.shape[1]
    inner = mine_ref[:, :rows]
    for ref in gots:
        inner = inner + ref[:, :rows].astype(F32)
    grads[...] = inner
    fetch.wait()
    a, b = near_rim(tab)
    for start, ref in ((a, from_a), (b, from_b)):
        grads[:, pl.ds(start, RIM)] = grads[:, pl.ds(start, RIM)] + ref[0].astype(F32)
    nblocks = blocks.shape[0] - 1
    for i in range(nblocks):
        cols = slice(i * BLK, (i + 1) * BLK)
        blocks[i] = (grads[:, cols] * slope_ref[:, cols]).astype(BF16).astype(F32)
    blocks[nblocks] = jnp.zeros_like(blocks[nblocks])
    spread(tab, blocks, spread_ref)
    part_slabs(ext_ref, spread_ref, keep_ref, send_ref, 7 * BLK)


def finish_body(counts, *refs):
    out_ref = refs[-1]
    depth = out_ref.shape[2]
    k = first = 0
    for count in counts:
        total = refs[first][...]
        for ref in refs[first + 1 : first + count]:
            total = total + ref[...].astype(F32)
        first += count
        for i in range(total.shape[1] // depth):
            out_ref[k] = total[:, i * depth : (i + 1) * depth]
            k += 1


def swap(value, axis, bits):
    return lax.ppermute(value, axis, [(i, i ^ bits) for i in range(lax.axis_size(axis))])


def swap_other(value):
    pairs = [(i, i + 1) for i in range(1, lax.axis_size("space") - 1, 2)]
    return lax.ppermute(value, "space", pairs + [(j, i) for i, j in pairs])


def local(features, kernel_map, block_count, weight_one, weight_two, cotangent):
    slabs, parts = lax.axis_size("space"), lax.axis_size("chan")
    pairs = parts // 2
    rows, depth = features.shape
    nblocks = rows // BLK
    reach = (nblocks + 2 * HB) * BLK
    offsets, entries = kernel_map.shape[1:3]
    wide = weight_one.shape[2]
    flat = offsets * depth
    share = wide // slabs
    order = [0, 1] + [v for j in range(1, pairs) for v in (2 * j, 2 * j + 1)]
    work = 2 * flat * wide * reach
    blocks = pltpu.VMEM((nblocks + 1, depth, BLK), F32)
    ext = pltpu.VMEM((wide, reach), BF16)
    spread_shape = (nblocks + 2 * HB, flat, BLK)

    def finish(*groups):
        total = call(
            functools.partial(finish_body, [len(g) for g in groups]),
            [jax.ShapeDtypeStruct((offsets, share, depth), F32)],
            [held(v) for g in groups for v in g],
            traffic=2 << 20,
        )[0]
        return total.transpose(0, 2, 1)

    def reduce_far(keep, got, after):
        width = keep.shape[2]
        mine, *sends = call(
            functools.partial(halve_body, "space"),
            [pltpu.VMEM((share, width), F32)] + [pltpu.VMEM((share, width), BF16)] * (slabs // 2 - 1),
            [held(keep), held(got)],
            traffic=2 << 20,
            after=after,
        )
        return [mine] + [swap(v, "space", 2 * (j + 1)) for j, v in enumerate(sends)]

    w_one = weight_one.reshape(flat, wide)
    w_two = weight_two.reshape(flat, wide)

    shard_t = features.T
    far = [swap(shard_t, "chan", 2 * j) for j in range(1, pairs)]
    cot = cotangent.T
    tab, spread_two, keep, send, own = call(
        input_grad_body,
        [
            pltpu.VMEM((entries + PAD, offsets), jnp.int32),
            pltpu.VMEM(spread_shape, BF16),
            pltpu.VMEM((pairs, depth, reach), BF16),
            pltpu.VMEM((pairs, depth, reach), BF16),
            pltpu.VMEM((depth, rows), BF16),
        ],
        [
            pltpu.with_memory_space_constraint(v, pltpu.HBM)
            for v in (block_count, kernel_map[0].transpose(2, 1, 0), cot, w_two, shard_t)
        ],
        [
            pltpu.VMEM((3, entries, offsets), jnp.int32),
            pltpu.VMEM(cot.shape, BF16),
            pltpu.VMEM(w_two.shape, BF16),
            blocks,
            pltpu.VMEM((parts, depth, reach), BF16),
            pltpu.SMEM((entries + PAD, offsets), jnp.int32),
            pltpu.SMEM(block_count.shape, jnp.int32),
            pltpu.SemaphoreType.DMA((5,)),
            pltpu.SemaphoreType.DMA,
        ],
        vmem=16,
        flops=work,
        traffic=16 << 20,
        specs=[FAR] * 5,
    )
    pieces = [own, swap(shard_t, "chan", 1)]
    for got in far:
        (got,) = call(pass_body, [pltpu.VMEM(got.shape, BF16)], [held(got)], after=[send])
        pieces += [got, swap(got, "chan", 1)]
    half_rim = pltpu.VMEM((wide // 2, RIM), BF16)
    rim_a, rim_b = call(
        functools.partial(cut_body, order),
        [half_rim, half_rim],
        [held(tab)] + [held(v) for v in pieces],
        [pltpu.VMEM((wide, RIM), BF16)],
        flops=8 * work,
    )
    x_a, x_b = swap(rim_a, "space", 1), swap_other(rim_b)
    got = swap(send, "chan", 1)
    mine, *sends = call(
        functools.partial(halve_body, "chan"),
        [pltpu.VMEM((depth, reach), F32)] + [pltpu.VMEM((depth, reach), BF16)] * (pairs - 1),
        [held(keep), held(got)],
        traffic=2 << 20,
        after=[rim_a],
    )
    gots = [swap(v, "chan", 2 * (j + 1)) for j, v in enumerate(sends)]

    table_scratch = [pltpu.SMEM((entries + PAD, offsets), jnp.int32), pltpu.SemaphoreType.DMA]
    conv_scratch = [ext, pltpu.VMEM(spread_shape, F32)] + table_scratch + [blocks] * 2
    prod_one, x_wide = call(
        functools.partial(inner_body, order),
        [pltpu.VMEM(spread_shape, F32), pltpu.VMEM((wide, rows), BF16)],
        [w_one] + [held(v) for v in pieces],
        vmem=10,
        flops=work,
        traffic=16 << 20,
        after=[mine],
    )
    (x_half,) = call(
        stack_body, [pltpu.VMEM((wide // 2, 2 * RIM), BF16)], [held(x_a), held(x_b)], after=[x_wide]
    )
    z_one, hidden, x_rims, _ = call(
        hidden_body,
        [pltpu.VMEM((depth, rows), F32), pltpu.VMEM((depth, rows), BF16), pltpu.VMEM((wide, 2 * RIM), BF16), pltpu.VMEM(spread_shape, F32)],
        [held(tab), w_one] + [held(v) for v in (x_half, swap(x_half, "chan", 1), prod_one)],
        table_scratch + [blocks] * 2,
        vmem=12,
        aliases={4: 3},
    )
    far = [swap(hidden, "chan", 2 * j) for j in range(1, pairs)]
    to_a, to_b = call(
        functools.partial(turn_body, len(gots)),
        [pltpu.VMEM((2, depth, RIM), BF16), pltpu.VMEM((2, depth, RIM), BF16)],
        [held(tab)] + [held(v) for v in [hidden, mine] + gots],
        traffic=2 << 20,
    )
    from_a, from_b = swap(to_a, "space", 1), swap_other(to_b)
    rim, full = call(
        pack_body,
        [pltpu.VMEM((depth, 2 * RIM), BF16), pltpu.VMEM((depth, reach), BF16)],
        [held(v) for v in (hidden, from_a, from_b)],
        traffic=1 << 20,
    )
    far_rims = [swap(rim, "chan", 2 * j) for j in range(1, pairs)]
    full_other = swap(full, "chan", 1)

    slope, x_ext = call(
        prepare_body,
        [pltpu.VMEM((depth, rows), F32), pltpu.VMEM((wide, reach), BF16)],
        [held(v) for v in (z_one, x_wide, x_rims)],
        after=[to_a],
    )
    keep_one, send_one = call(
        functools.partial(grad_one_body, len(gots)),
        [pltpu.VMEM((slabs // 2, share, flat), F32), pltpu.VMEM((slabs // 2, share, flat), BF16)],
        [held(tab)] + [held(v) for v in [slope, from_a, from_b, x_ext, mine] + gots],
        [pltpu.VMEM((depth, rows), F32), blocks, pltpu.VMEM(spread_shape, BF16)] + table_scratch,
        vmem=24,
        flops=work,
        traffic=16 << 20,
    )
    got_one = swap(send_one, "space", 1)

    pieces = [full, full_other]
    for got, got_rim in zip(far, far_rims):
        (got,) = call(
            append_body, [pltpu.VMEM((depth, reach), BF16)], [held(got), held(got_rim)], traffic=1 << 20, after=[keep_one]
        )
        pieces += [got, swap(got, "chan", 1)]
    cut = min(Y_FIRST, offsets) * depth
    far_part = (2, share, flat - cut)
    keep_two, send_two, mine_far, *sends_far = call(
        functools.partial(grad_two_body, order),
        [
            pltpu.VMEM((slabs // 2, share, cut), F32),
            pltpu.VMEM((slabs // 2, share, cut), BF16),
            pltpu.VMEM(far_part, F32),
        ]
        + [pltpu.VMEM(far_part, BF16)] * (slabs // 2 - 1),
        [held(v) for v in [spread_two] + pieces],
        [ext, pltpu.VMEM((slabs // 2,) + far_part, F32)],
        vmem=14,
        flops=work // 4,
    )
    gots_far = [swap(v, "space", 2 * (j + 1)) for j, v in enumerate(sends_far)]
    got_two = swap(send_two, "space", 1)
    group_one = reduce_far(keep_one, got_one, [])
    output, done = call(
        functools.partial(output_body, order),
        [jax.ShapeDtypeStruct((depth, rows), BF16), pltpu.VMEM((8, BLK), F32)],
        [held(tab), w_two] + [held(v) for v in pieces],
        conv_scratch,
        vmem=34,
        flops=8 * work,
        traffic=16 << 20,
        after=[group_one[0]],
    )
    keep_far, send_far = call(
        functools.partial(split_body, len(gots_far)),
        [pltpu.VMEM(far_part[1:], F32), pltpu.VMEM(far_part[1:], BF16)],
        [held(v) for v in [mine_far] + gots_far],
        traffic=1 << 20,
        after=[done],
    )
    got_far = swap(send_far, "space", 1)
    group_two = reduce_far(keep_two, got_two, [keep_far])
    grad_one = finish(group_one)
    grad_two = finish(group_two, [keep_far, got_far])
    return output.T, grad_one, grad_two


def solution(mesh):
    return jax.shard_map(
        local,
        mesh=mesh,
        in_specs=(
            P("space", "chan"),
            P("space", None, None, None),
            P(),
            P(None, "chan", None),
            P(None, "chan", None),
            P("space", "chan"),
        ),
        out_specs=(P("space", "chan"), P(None, "chan", "space"), P(None, "chan", "space")),
        check_vma=False,
    )
```
